256 devices in a mesh: lon: 16 (over y_lo, x, core), lat: 16 (over y_hi, z).
Axes of the slice: x: 4, y: 4 (y_hi: 2, y_lo: 2; y = y_hi * 2 + y_lo), z: 8, core: 2. Of those that a mesh axis runs over, the one named last changes fastest.
Arguments:
- tokens: bfloat16 [2, 192, 384, 192], P(None, 'lat', 'lon'), may hold values from -6 to 6
- gain_attn_first: float32 [192], replicated, may hold values from 0.1 to 1.9
- qkv_first: bfloat16 [192, 576], replicated, may hold values from -0.4375 to 0.4375
- proj_first: bfloat16 [192, 192], replicated, may hold values from -0.4375 to 0.4375
- gain_mlp_first: float32 [192], replicated, may hold values from 0.1 to 1.9
- up_first: bfloat16 [192, 768], replicated, may hold values from -0.4375 to 0.4375
- down_first: bfloat16 [768, 192], replicated, may hold values from -0.21875 to 0.21875
- bias_first: bfloat16 [32, 1, 6, 144, 144], P('lat'), may hold values from -6 to 6
- gain_attn_second: float32 [192], replicated, may hold values from 0.1 to 1.9
- qkv_second: bfloat16 [192, 576], replicated, may hold values from -0.4375 to 0.4375
- proj_second: bfloat16 [192, 192], replicated, may hold values from -0.4375 to 0.4375
- gain_mlp_second: float32 [192], replicated, may hold values from 0.1 to 1.9
- up_second: bfloat16 [192, 768], replicated, may hold values from -0.4375 to 0.4375
- down_second: bfloat16 [768, 192], replicated, may hold values from -0.21875 to 0.21875
- bias_second: bfloat16 [32, 1, 6, 144, 144], P('lat'), may hold values from -6 to 6
- cotangent: bfloat16 [2, 192, 384, 192], P(None, 'lat', 'lon'), may hold values from -6 to 6
Outputs:
- result: bfloat16 [2, 192, 384, 192], P(None, 'lat', 'lon')
- grad_tokens: bfloat16 [2, 192, 384, 192], P(None, 'lat', 'lon')
- grad_qkv_first: float32 [192, 576], replicated
- grad_proj_first: float32 [192, 192], replicated
- grad_up_first: float32 [192, 768], replicated
- grad_down_first: float32 [768, 192], replicated
- grad_qkv_second: float32 [192, 576], replicated
- grad_proj_second: float32 [192, 192], replicated
- grad_up_second: float32 [192, 768], replicated
- grad_down_second: float32 [768, 192], replicated
The draws below stay inside these ranges and needn't reach their ends.
All inputs are finite; a program needn't handle non-finite values.
Results may differ from the reference program's by a relative error of at most 0.025.
Values may be sent and summed in bfloat16 or wider, within the bound.
A program may use at most 128 MiB of HBM per device.

```python
import math
import jax
import jax.numpy as jnp
from jax import lax

D = 192
HEADS = 6
HIDDEN_SIZE = 768
WZ = 2
WLAT = 6
WLON = 12
LEVELS = 2
PAD = 11
NLAT = 192
NLON = 384
WIN = 144
TOKENS = 147456


def shard_levels(own_key, shape, shards, smallest, top_value):
    factor_of = 1.0
    for dim, parts in shards:
        draws = jax.random.uniform(jax.random.fold_in(jax.random.fold_in(own_key, 6), dim), (parts,), jnp.float32, smallest / len(shards), top_value / len(shards))
        factor_of = factor_of * jnp.repeat(jnp.exp(draws), shape[dim] // parts).reshape((-1,) + (1,) * (len(shape) - 1 - dim))
    return factor_of


def noise(own_key, shape, width, bound, pieces=(), kind=jnp.bfloat16):
    drawn = width * jax.random.normal(own_key, shape, jnp.float32)
    if pieces:
        drawn = drawn * shard_levels(own_key, shape, pieces, -0.22, 0.18)
    return jnp.clip(drawn, -bound, bound).astype(kind)


def setup_inputs(seed: int = 0) -> dict:
    seeds = jax.random.split(jax.random.key(seed), 17)
    return {
        "tokens": noise(seeds[0], (LEVELS, NLAT, NLON, D), 1.0, 6.0, ((1, 16), (2, 16))),
        "gain_attn_first": jnp.clip(1.0 + 0.18 * jax.random.normal(seeds[1], (D,), jnp.float32), 0.1, 1.9),
        "qkv_first": noise(seeds[2], (D, 3 * D), D ** -0.5, 0.4375),
        "proj_first": noise(seeds[3], (D, D), D ** -0.5, 0.4375),
        "gain_mlp_first": jnp.clip(1.0 + 0.18 * jax.random.normal(seeds[4], (D,), jnp.float32), 0.1, 1.9),
        "up_first": noise(seeds[5], (D, HIDDEN_SIZE), D ** -0.5, 0.4375),
        "down_first": noise(seeds[6], (HIDDEN_SIZE, D), HIDDEN_SIZE ** -0.5, 0.21875),
        "bias_first": noise(seeds[7], (NLAT // WLAT, LEVELS // WZ, HEADS, WIN, WIN), 1.0, 6.0, ((0, 16),)),
        "gain_attn_second": jnp.clip(1.0 + 0.18 * jax.random.normal(seeds[8], (D,), jnp.float32), 0.1, 1.9),
        "qkv_second": noise(seeds[9], (D, 3 * D), D ** -0.5, 0.4375),
        "proj_second": noise(seeds[10], (D, D), D ** -0.5, 0.4375),
        "gain_mlp_second": jnp.clip(1.0 + 0.18 * jax.random.normal(seeds[11], (D,), jnp.float32), 0.1, 1.9),
        "up_second": noise(seeds[12], (D, HIDDEN_SIZE), D ** -0.5, 0.4375),
        "down_second": noise(seeds[13], (HIDDEN_SIZE, D), HIDDEN_SIZE ** -0.5, 0.21875),
        "bias_second": noise(seeds[14], (NLAT // WLAT, LEVELS // WZ, HEADS, WIN, WIN), 1.0, 6.0, ((0, 16),)),
        "cotangent": noise(seeds[15], (LEVELS, NLAT, NLON, D), 1.0, 6.0, ((1, 16), (2, 16))),
    }


def layer_norm(values, norm_gain):
    row_mean = lax.optimization_barrier(jnp.mean(values, axis=-1, keepdims=True))
    centred = values - row_mean
    row_var = lax.optimization_barrier(jnp.mean(centred * centred, axis=-1, keepdims=True))
    return centred * lax.rsqrt(row_var + 1e-05) * norm_gain.astype(jnp.float32)

def to_windows(field, head_count):
    level_count, row_count, col_count, feat_width = field.shape
    head_size = feat_width // head_count
    split = field.reshape(level_count // WZ, WZ, row_count // WLAT, WLAT, col_count // WLON, WLON, head_count, head_size)
    moved = split.transpose(2, 0, 4, 6, 1, 3, 5, 7)
    return moved.reshape(row_count // WLAT, level_count // WZ, col_count // WLON, head_count, WZ * WLAT * WLON, head_size)

def from_windows(field, level_count, row_count, col_count):
    head_count = field.shape[3]
    head_size = field.shape[5]
    split = field.reshape(row_count // WLAT, level_count // WZ, col_count // WLON, head_count, WZ, WLAT, WLON, head_size)
    moved = split.transpose(1, 4, 0, 5, 2, 6, 3, 7)
    return moved.reshape(level_count, row_count, col_count, head_count * head_size)

def run_block(patch_in, row_start, row_limit, gain_attn, w_qkv, w_proj, gain_mlp, w_up, w_down, bias):
    level_count, row_count, col_count, feat_width = patch_in.shape
    head_count = bias.shape[2]
    head_size = feat_width // head_count
    row_pos = row_start + jnp.arange(row_count, dtype=jnp.int32)
    row_valid = ((row_pos >= 0) & (row_pos < row_limit)).astype(jnp.float32)
    resid_in = patch_in.astype(jnp.float32)
    normed = layer_norm(resid_in, gain_attn).astype(jnp.bfloat16)
    projected = jnp.dot(normed.astype(jnp.float32), w_qkv, precision=lax.Precision.HIGHEST).astype(jnp.bfloat16)
    query_win = to_windows(projected[..., :feat_width], head_count)
    key_win = to_windows(projected[..., feat_width:2 * feat_width], head_count)
    value_win = to_windows(projected[..., 2 * feat_width:], head_count)
    key_rows = row_valid.reshape(row_count // WLAT, WLAT)
    key_mask = jnp.broadcast_to(key_rows[:, None, :, None], (row_count // WLAT, WZ, WLAT, WLON))
    key_mask = key_mask.reshape(row_count // WLAT, 1, 1, 1, 1, WZ * WLAT * WLON)
    penalty = (key_mask - 1.0) * 30000.0
    scores = jnp.einsum('caegqh,caegkh->caegqk', query_win.astype(jnp.float32), key_win.astype(jnp.float32))
    scores = scores * head_size ** (-0.5) + bias[:, :, None].astype(jnp.float32) + penalty
    soft_weights = jax.nn.softmax(scores, axis=-1).astype(jnp.bfloat16)
    attended = jnp.einsum('caegqk,caegkh->caegqh', soft_weights.astype(jnp.float32), value_win.astype(jnp.float32)).astype(jnp.bfloat16)
    merged = from_windows(attended, level_count, row_count, col_count)
    residual = resid_in + jnp.dot(merged.astype(jnp.float32), w_proj, precision=lax.Precision.HIGHEST)
    second = layer_norm(residual, gain_mlp).astype(jnp.bfloat16)
    hidden = jax.nn.gelu(jnp.dot(second.astype(jnp.float32), w_up, precision=lax.Precision.HIGHEST)).astype(jnp.bfloat16)
    block_out = residual + jnp.dot(hidden.astype(jnp.float32), w_down, precision=lax.Precision.HIGHEST)
    return (block_out * row_valid[None, :, None, None]).astype(jnp.bfloat16)

def roll_in(field):
    half_lat = WLAT // 2
    half_lon = WLON // 2
    rolled = jnp.roll(field, half_lon, axis=2)
    return jnp.concatenate([jnp.zeros_like(rolled[:, :half_lat]), rolled[:, :-half_lat]], axis=1)

def roll_out(field):
    half_lat = WLAT // 2
    half_lon = WLON // 2
    moved = jnp.concatenate([field[:, half_lat:], jnp.zeros_like(field[:, :half_lat])], axis=1)
    return jnp.roll(moved, -half_lon, axis=2)

def reference(tokens, gain_attn_first, qkv_first, proj_first, gain_mlp_first, up_first, down_first, bias_first, gain_attn_second, qkv_second, proj_second, gain_mlp_second, up_second, down_second, bias_second, cotangent):
    row_limit = NLAT - PAD
    half_lat = WLAT // 2

    def forward(inputs, first_mats, second_mats):
        first = run_block(inputs, 0, row_limit, gain_attn_first, first_mats[0], first_mats[1], gain_mlp_first, first_mats[2], first_mats[3], bias_first)
        shifted = roll_in(first)
        second = run_block(shifted, -half_lat, row_limit, gain_attn_second, second_mats[0], second_mats[1], gain_mlp_second, second_mats[2], second_mats[3], bias_second)
        return roll_out(second)
    first_mats = (qkv_first.astype(jnp.float32), proj_first.astype(jnp.float32), up_first.astype(jnp.float32), down_first.astype(jnp.float32))
    second_mats = (qkv_second.astype(jnp.float32), proj_second.astype(jnp.float32), up_second.astype(jnp.float32), down_second.astype(jnp.float32))
    result, pull_back = jax.vjp(forward, tokens, first_mats, second_mats)
    grad_tokens, grads_first, grads_second = pull_back(cotangent)
    grad_scale = 1.0 / math.sqrt(float(TOKENS))
    return (result, grad_tokens, grads_first[0] * grad_scale, grads_first[1] * grad_scale, grads_first[2] * grad_scale, grads_first[3] * grad_scale, grads_second[0] * grad_scale, grads_second[1] * grad_scale, grads_second[2] * grad_scale, grads_second[3] * grad_scale)
```

```python
import functools
import math

import jax
import jax.numpy as jnp
from jax import lax
from jax.experimental import pallas as pl
from jax.experimental.pallas import tpu as pltpu
from jax.sharding import PartitionSpec as P

F32 = jnp.float32
BF16 = jnp.bfloat16
HEADS = 6
WIN = 144
PAD = 11
D = 192
STACK = 896
SCALE = 32 ** -0.5
CHUNKS = ((0, 256), (256, 512), (512, 768), (768, 896))
PIECE = 112
HALF = 16 * PIECE
ROWS = 2 * HALF
MESH = pl.DeviceIdType.MESH


def dot_nn(a, b):
    return lax.dot_general(a, b, (((1,), (0,)), ((), ())), preferred_element_type=F32)


def dot_nt(a, b):
    return lax.dot_general(a, b, (((1,), (1,)), ((), ())), preferred_element_type=F32)


def dot_tn(a, b):
    return lax.dot_general(a, b, (((0,), (0,)), ((), ())), preferred_element_type=F32)


def win_rows(w):
    return pl.ds(pl.multiple_of(w * WIN, 16), WIN)


def normalise(x):
    mean = jnp.mean(x, axis=-1, keepdims=True)
    centred = x - mean
    var = jnp.mean(centred * centred, axis=-1, keepdims=True)
    r = lax.rsqrt(var + 1e-05)
    return centred * r, r


def normalise_back(dy, xhat, r):
    m1 = jnp.mean(dy, axis=-1, keepdims=True)
    m2 = jnp.mean(dy * xhat, axis=-1, keepdims=True)
    return r * (dy - m1 - xhat * m2)


def live_column(first_row, limit):
    n = lax.broadcasted_iota(jnp.int32, (WIN, 1), 0)
    m = jnp.where(n >= 72, n - 72, n)
    row = jnp.zeros_like(m)
    for i in range(1, 6):
        row = row + jnp.where(m >= 12 * i, 1, 0)
    pos = row + first_row
    return jnp.where((pos >= 0) & (pos < limit), 1.0, 0.0).astype(F32)


def head_mask(h, dtype):
    lane = lax.broadcasted_iota(jnp.int32, (1, D), 1)
    inside = (lane >= 32 * h) & (lane < 32 * h + 32)
    return jnp.where(inside, 1.0, 0.0).astype(F32).astype(dtype)


def tile_to_windows(src, dst):
    for level in range(2):
        for row in range(12):
            x = src[level * 12 + row].astype(F32)
            for wc in range(2):
                at = ((row // 6) * 2 + wc) * WIN + level * 72 + (row % 6) * 12
                dst[at : at + 12, :] = x[12 * wc : 12 * wc + 12, :]


def windows_to_tile(src, dst):
    for level in range(2):
        for row in range(12):
            parts = []
            for wc in range(2):
                at = ((row // 6) * 2 + wc) * WIN + level * 72 + (row % 6) * 12
                parts.append(src[at : at + 12, :])
            dst[level * 12 + row] = jnp.concatenate(parts, axis=0).astype(BF16)


def place(level, row, col):
    return ((row // 6) * 2 + col // 12) * WIN + level * 72 + (row % 6) * 12 + col % 12


def pack_halo(src, pack, out, row0, row1, col0, col1):
    at = 0
    for rows, cols in ((row0, col1), (row1, col0), (row1, col1)):
        for level in range(2):
            for row in rows:
                for col in cols:
                    p = place(level, row, col)
                    pack[at : at + 6, :] = src[p : p + 6, :]
                    at += 6
        at = (at + 15) // 16 * 16
    out[...] = pack[...].astype(BF16)


HALO_ROWS = 112 + 112 + 48
HALO_PARTS = ((0, 112), (112, 112), (224, 48))


def unpack_shift(src, halo, dst, step):
    for level in range(2):
        for row in range(12):
            for col in range(0, 24, 6):
                r, c = row - 3 * step, col - 6 * step
                r_in, c_in = 0 <= r < 12, 0 <= c < 24
                if r_in and c_in:
                    p = place(level, r, c)
                    piece = src[p : p + 6, :]
                else:
                    if r_in:
                        i = r if step > 0 else r - 3
                        at = (level * 9 + i) * 6
                    elif c_in:
                        i = row if step > 0 else row - 9
                        j = c if step > 0 else c - 6
                        at = 112 + (level * 3 + i) * 18 + j
                    else:
                        i = row if step > 0 else row - 9
                        at = 224 + (level * 3 + i) * 6
                    piece = halo[at : at + 6, :]
                q = place(level, row, col)
                dst[q : q + 6, :] = piece


def megakernel(
    tok, ct,
    ga1, qkv1, proj1, gm1, up1, dn1, bias1,
    ga2, qkv2, proj2, gm2, up2, dn2, bias2,
    res_o, gt_o, f_o,
    wp, bt, xhat1, r1, normed, proj_all, qm, pt, att, xhat2, r2, second, hidden, gp,
    cur, nxt, cw, pack, halo_f, halo_out, halo_in,
    dtot, du, dres, dres_b, datt, dom, dst_, dqkv, w6,
    g, r0, hh, rr1, z, rr2, zg, f,
    halo_send, halo_recv, core_send, core_recv, xy_send, xy_recv, z_send, z_recv,
    zg_send, zg_recv, ag_send, ag_recv, fw_send, fw_recv, out_sem,
):
    lon = lax.axis_index("lon")
    lat = lax.axis_index("lat")
    core = lax.rem(lon, 2)
    chip = lon // 2
    y_hi = lat // 8
    zi = lax.rem(lat, 8)
    me_xy = y_hi * 8 + chip

    def sibling():
        return {"lon": chip * 2 + 1 - core, "lat": lat}

    def xy_dev(j):
        return {"lon": lax.rem(j, 8) * 2 + core, "lat": (j // 8) * 8 + zi}

    def z_dev(j):
        return {"lon": lon, "lat": y_hi * 8 + j}

    def near(step_lon, step_lat):
        return {
            "lon": lax.rem(lon + step_lon + 16, 16),
            "lat": lax.rem(lat + step_lat + 16, 16),
        }

    barrier = pltpu.get_barrier_semaphore()

    def greet(device):
        pl.semaphore_signal(barrier, inc=1, device_id=device, device_id_type=MESH)

    greet(sibling())
    for k in range(1, 16):
        greet(xy_dev(lax.rem(me_xy + k, 16)))
    for k in range(1, 8):
        greet(z_dev(lax.rem(zi + k, 8)))
    for s in (1, -1):
        greet(near(s, 0))
        greet(near(0, s))
        greet(near(s, s))

    def halo_copy(x, part, step):
        first, count = HALO_PARTS[part]
        device = near(step if part != 1 else 0, step if part != 0 else 0)
        return pltpu.make_async_remote_copy(
            src_ref=halo_out.at[x, pl.ds(first, count)],
            dst_ref=halo_in.at[x, pl.ds(first, count)],
            send_sem=halo_send.at[x, part],
            recv_sem=halo_recv.at[x, part],
            device_id=device,
            device_id_type=MESH,
        )

    def halo_start(x, src, step):
        if step > 0:
            pack_halo(src, pack, halo_out.at[x], range(0, 9), range(9, 12), (0, 6, 12), (18,))
        else:
            pack_halo(src, pack, halo_out.at[x], range(3, 12), range(0, 3), (6, 12, 18), (0,))
        for part in range(3):
            halo_copy(x, part, step).start()

    def halo_finish(x, src, dst, step):
        for part in range(3):
            halo_copy(x, part, step).wait()
        outside = jnp.where(lat == (0 if step > 0 else 15), 0.0, 1.0).astype(F32)
        halo_f[0:112, :] = halo_in[x, 0:112].astype(F32)
        halo_f[112:, :] = halo_in[x, 112:].astype(F32) * outside
        unpack_shift(src, halo_f, dst, step)

    limit = 16 * 12 - PAD
    starts = (lat * 12, lat * 12 - 3)
    weights = (
        (ga1, qkv1, proj1, gm1, up1, dn1, bias1),
        (ga2, qkv2, proj2, gm2, up2, dn2, bias2),
    )

    def live(b, w):
        return live_column(starts[b] + 6 * (w // 2), limit)

    def block_forward(b, x_in, x_out):
        ga, wqkv, wproj, gm, wup, wdn, bias = weights[b]
        wp[b] = jnp.zeros((D, 768), BF16)
        for i in range(3):
            part = wqkv[...].astype(F32)[:, D * i : D * i + D]
            wp[b, :, 256 * i : 256 * i + D] = part.astype(BF16)
        rows_i = lax.broadcasted_iota(jnp.int32, (WIN, WIN), 0)
        cols_i = lax.broadcasted_iota(jnp.int32, (WIN, WIN), 1)
        eye = jnp.where(rows_i == cols_i, 1.0, 0.0).astype(F32).astype(BF16)
        for wr in range(2):
            penalty = (live_column(starts[b] + 6 * wr, limit) - 1.0) * 30000.0
            bt[wr, :, 0:864] = dot_nt(eye, bias[wr]) + penalty
            bt[wr, :, 864:] = jnp.zeros((WIN, STACK - 864), F32)
        gain_a = ga[...].reshape(1, D)
        gain_m = gm[...].reshape(1, D)

        @pl.loop(0, 4)
        def _(w):
            rows = win_rows(w)
            xh, r = normalise(x_in[rows, :])
            xhat1[b, rows, :] = xh
            r1[b, rows, :] = r
            nb = (xh * gain_a).astype(BF16)
            normed[b, rows, :] = nb
            proj_all[b, rows, :] = dot_nn(nb, wp[b]).astype(BF16)

        @pl.loop(0, 4)
        def _(w):
            rows = win_rows(w)
            wr = w // 2
            q = proj_all[b, rows, 0:D]
            k = proj_all[b, rows, 256 : 256 + D]
            v = proj_all[b, rows, 512 : 512 + D]
            for h in range(HEADS):
                qm[b, w, WIN * h : WIN * h + WIN, :] = q * head_mask(h, BF16)
            qm[b, w, 864:, :] = jnp.zeros((STACK - 864, D), BF16)
            for c0, c1 in CHUNKS:
                s = dot_nt(k, qm[b, w, c0:c1, :]) * SCALE + bt[wr, :, c0:c1]
                e = jnp.exp(s - jnp.max(s, axis=0, keepdims=True))
                total = jnp.sum(e, axis=0, keepdims=True)
                pt[b, w, :, c0:c1] = (e * (1.0 / total)).astype(BF16)
            o = dot_tn(pt[b, w], v)
            a = jnp.zeros((WIN, D), F32)
            for h in range(HEADS):
                a = a + o[WIN * h : WIN * h + WIN, :] * head_mask(h, F32)
            att[b, rows, :] = a.astype(BF16)

        @pl.loop(0, 4)
        def _(w):
            rows = win_rows(w)
            resid = x_in[rows, :] + dot_nn(att[b, rows, :], wproj[...])
            xh, r = normalise(resid)
            xhat2[b, rows, :] = xh
            r2[b, rows, :] = r
            sb = (xh * gain_m).astype(BF16)
            second[b, rows, :] = sb
            u = dot_nn(sb, wup[...])
            c = math.sqrt(2.0 / math.pi)
            u2 = u * u
            t = jnp.tanh(u * (c + (c * 0.044715) * u2))
            half = 0.5 + 0.5 * t
            hb = (u * half).astype(BF16)
            hidden[b, rows, :] = hb
            slope = half + u * (0.5 - 0.5 * t * t) * (c + (3 * c * 0.044715) * u2)
            gp[b, rows, :] = slope.astype(BF16)
            out = (resid + dot_nn(hb, wdn[...])) * live(b, w)
            x_out[rows, :] = out.astype(BF16).astype(F32)

    def block_backward(b, d_out, d_in):
        ga, wqkv, wproj, gm, wup, wdn, bias = weights[b]
        gain_a = ga[...].reshape(1, D)
        gain_m = gm[...].reshape(1, D)

        @pl.loop(0, 4)
        def _(w):
            rows = win_rows(w)
            dt = d_out[rows, :] * live(b, w)
            dtb = dt.astype(BF16)
            dtot[rows, :] = dtb
            dh = dot_nt(dtb, wdn[...]).astype(BF16).astype(F32)
            dub = (dh * gp[b, rows, :].astype(F32)).astype(BF16)
            du[rows, :] = dub
            dy = dot_nt(dub, wup[...]).astype(BF16).astype(F32) * gain_m
            dr = dt + normalise_back(dy, xhat2[b, rows, :], r2[b, rows, :])
            dres[rows, :] = dr
            drb = dr.astype(BF16)
            dres_b[rows, :] = drb
            datt[rows, :] = dot_nt(drb, wproj[...]).astype(BF16)

        @pl.loop(0, 4)
        def _(w):
            rows = win_rows(w)
            k = proj_all[b, rows, 256 : 256 + D]
            v = proj_all[b, rows, 512 : 512 + D]
            do = datt[rows, :]
            for h in range(HEADS):
                dom[WIN * h : WIN * h + WIN, :] = do * head_mask(h, BF16)
            dom[864:, :] = jnp.zeros((STACK - 864, D), BF16)
            for c0, c1 in CHUNKS:
                dp = dot_nt(v, dom[c0:c1, :]).astype(BF16).astype(F32)
                p = pt[b, w, :, c0:c1].astype(F32)
                delta = jnp.sum(p * dp, axis=0, keepdims=True)
                dst_[:, c0:c1] = (p * (dp - delta)).astype(BF16)
            zeros = jnp.zeros((WIN, 64), BF16)
            dqkv[rows, 512 : 512 + D] = dot_nn(pt[b, w], dom[...]).astype(BF16)
            dqkv[rows, 256 : 256 + D] = (dot_nn(dst_[...], qm[b, w]) * SCALE).astype(BF16)
            o = dot_tn(dst_[...], k)
            a = jnp.zeros((WIN, D), F32)
            for h in range(HEADS):
                a = a + o[WIN * h : WIN * h + WIN, :] * head_mask(h, F32)
            dqkv[rows, 0:D] = (a * SCALE).astype(BF16)
            for i in range(3):
                dqkv[rows, 256 * i + D : 256 * i + 256] = zeros

        @pl.loop(0, 4)
        def _(w):
            rows = win_rows(w)
            dy = dot_nt(dqkv[rows, :], wp[b]).astype(BF16).astype(F32) * gain_a
            dx = dres[rows, :] + normalise_back(dy, xhat1[b, rows, :], r1[b, rows, :])
            d_in[rows, :] = dx.astype(BF16).astype(F32)

    def weight_terms(b):
        w6[...] = dot_tn(normed[b], dqkv[...])
        pr = dot_tn(att[b], dres_b[...])
        for i in range(3):
            w6[:, 256 * i + D : 256 * i + 256] = pr[:, 64 * i : 64 * i + 64]
        for i in range(6):
            g[b, i * D : i * D + D, :] = w6[:, 128 * i : 128 * i + 128].astype(BF16)
        gu = dot_tn(second[b], du[...])
        for i in range(6):
            g[b, (6 + i) * D : (7 + i) * D, :] = gu[:, 128 * i : 128 * i + 128].astype(BF16)
        gd = dot_tn(dtot[...], hidden[b])
        for i in range(6):
            g[b, (12 + i) * D : (13 + i) * D, :] = gd[:, 128 * i : 128 * i + 128].astype(BF16)
        g[b, 18 * D :, :] = jnp.zeros((ROWS - 18 * D, 128), BF16)

    def remote(src, dst, send, recv, device):
        return pltpu.make_async_remote_copy(
            src_ref=src, dst_ref=dst, send_sem=send, recv_sem=recv,
            device_id=device, device_id_type=MESH,
        )

    def half_at(c):
        return pl.ds(pl.multiple_of(c * HALF, 16), HALF)

    def piece_at(j):
        return pl.ds(pl.multiple_of(j * PIECE, 16), PIECE)

    def f_at(j):
        return pl.ds(pl.multiple_of(core * HALF + j * PIECE, 16), PIECE)

    def tile_at(j):
        return pl.ds(pl.multiple_of(j * 16, 16), 16)

    def core_copy(b):
        return remote(g.at[b, half_at(1 - core)], r0.at[b], core_send.at[b], core_recv.at[b], sibling())

    def xy_copy(b, j, slot):
        return remote(hh.at[b, piece_at(j)], rr1.at[b, slot], xy_send.at[b, j], xy_recv.at[b, slot], xy_dev(j))

    def z_copy(b, j, slot):
        return remote(z.at[b, tile_at(j)], rr2.at[b, slot], z_send.at[b, j], z_recv.at[b, slot], z_dev(j))

    def zg_copy(b, j, slot):
        return remote(zg.at[b, tile_at(slot)], zg.at[b, tile_at(slot)], zg_send.at[b, j], zg_recv.at[b, slot], z_dev(j))

    def ag_copy(b, j, slot):
        return remote(f.at[b, f_at(slot)], f.at[b, f_at(slot)], ag_send.at[b, j], ag_recv.at[b, slot], xy_dev(j))

    def fw_copy(b, j):
        return remote(f.at[b, f_at(j)], f.at[b, f_at(j)], fw_send.at[b, j], fw_recv.at[b, j], sibling())

    def fw_arrived(b, j):
        other = pl.ds(pl.multiple_of((1 - core) * HALF + j * PIECE, 16), PIECE)
        return remote(f.at[b, other], f.at[b, other], fw_send.at[b, j], fw_recv.at[b, j], sibling())

    def xy_others(body):
        def step(k, carry):
            body(lax.rem(me_xy + k, 16))
            return carry
        lax.fori_loop(1, 16, step, 0)

    def z_others(body):
        def step(k, carry):
            body(lax.rem(zi + k, 8))
            return carry
        lax.fori_loop(1, 8, step, 0)

    def sum_0(b):
        core_copy(b).start()

    def sum_1(b):
        core_copy(b).wait()
        def step(j, carry):
            own = g[b, pl.ds(pl.multiple_of(core * HALF + j * PIECE, 16), PIECE), :].astype(F32)
            hh[b, piece_at(j), :] = (own + r0[b, piece_at(j), :].astype(F32)).astype(BF16)
            return carry
        lax.fori_loop(0, 16, step, 0)
        xy_others(lambda j: xy_copy(b, j, me_xy).start())

    def sum_2(b):
        xy_others(lambda j: xy_copy(b, me_xy, j).wait_recv())
        rr1[b, me_xy] = hh[b, piece_at(me_xy), :]
        total = lax.fori_loop(
            0, 16, lambda j, a: a + rr1[b, j].astype(F32), jnp.zeros((PIECE, 128), F32)
        )
        z[b, 0:PIECE, :] = total.astype(BF16)
        z[b, PIECE:, :] = jnp.zeros((16, 128), BF16)
        z_others(lambda j: z_copy(b, j, zi).start())

    def sum_3(b):
        z_others(lambda j: z_copy(b, zi, j).wait_recv())
        rr2[b, zi] = z[b, tile_at(zi), :]
        total = jnp.zeros((16, 128), F32)
        for j in range(8):
            total = total + rr2[b, j].astype(F32)
        zg[b, tile_at(zi), :] = total.astype(BF16)
        z_others(lambda j: zg_copy(b, j, zi).start())

    def sum_4(b):
        z_others(lambda j: zg_copy(b, zi, j).wait_recv())
        f[b, f_at(me_xy), :] = zg[b, 0:PIECE, :]
        xy_others(lambda j: ag_copy(b, j, me_xy).start())
        fw_copy(b, me_xy).start()

    def sum_5(b):
        def forward(j):
            ag_copy(b, me_xy, j).wait_recv()
            fw_copy(b, j).start()
        xy_others(forward)

    def sum_6(b):
        def arrived(j, carry):
            fw_arrived(b, j).wait_recv()
            fw_copy(b, j).wait_send()
            return carry
        lax.fori_loop(0, 16, arrived, 0)
        def sent(j):
            xy_copy(b, j, me_xy).wait_send()
            ag_copy(b, j, me_xy).wait_send()
        xy_others(sent)
        def sent_z(j):
            z_copy(b, j, zi).wait_send()
            zg_copy(b, j, zi).wait_send()
        z_others(sent_z)

    tile_to_windows(tok, cur)
    tile_to_windows(ct, cw)
    pl.semaphore_wait(barrier, 29)
    halo_start(0, cw, 1)
    block_forward(0, cur, nxt)
    halo_start(1, nxt, 1)
    halo_finish(1, nxt, cur, 1)
    block_forward(1, cur, nxt)
    halo_start(2, nxt, -1)
    halo_finish(0, cw, cur, 1)
    block_backward(1, cur, cw)
    halo_start(3, cw, -1)
    weight_terms(1)
    sum_0(1)
    halo_finish(2, nxt, cur, -1)
    windows_to_tile(cur, res_o)
    halo_finish(3, cw, nxt, -1)
    block_backward(0, nxt, cur)
    weight_terms(0)
    windows_to_tile(cur, gt_o)
    sum_0(0)
    sum_1(1)
    sum_1(0)
    sum_2(1)
    sum_2(0)
    sum_3(1)
    sum_3(0)
    sum_4(1)
    sum_4(0)
    sum_5(1)
    sum_5(0)
    sum_6(1)
    sum_6(0)
    out = pltpu.make_async_copy(f, f_o, out_sem)
    out.start()
    out.wait()


def unpack_kernel(factor, f, res, gt, res_o, gt_o, *outs):
    res_o[...] = res[...]
    gt_o[...] = gt[...]
    for b in range(2):
        qkv, proj, up, down = outs[4 * b : 4 * b + 4]

        def tile(i):
            return f[b, i * D : i * D + D, :].astype(F32) * factor

        for i in range(3):
            two = jnp.concatenate([tile(2 * i), tile(2 * i + 1)], axis=1)
            qkv[:, D * i : D * i + D] = two[:, 0:D]
            proj[:, 64 * i : 64 * i + 64] = two[:, D:]
        for i in range(6):
            up[:, 128 * i : 128 * i + 128] = tile(6 + i)
            down[128 * i : 128 * i + 128, :] = tile(12 + i).T


def body(
    tokens, ga1, qkv1, proj1, gm1, up1, dn1, bias1,
    ga2, qkv2, proj2, gm2, up2, dn2, bias2, cotangent,
):
    vmem = pl.BlockSpec(memory_space=pltpu.VMEM)
    tile = jax.ShapeDtypeStruct((24, 24, D), BF16)

    def dma(*shape):
        return pltpu.SemaphoreType.DMA(shape)

    scratch = [
        pltpu.VMEM((2, D, 768), BF16),
        pltpu.VMEM((2, WIN, STACK), F32),
        pltpu.VMEM((2, 576, D), F32),
        pltpu.VMEM((2, 576, 1), F32),
        pltpu.VMEM((2, 576, D), BF16),
        pltpu.VMEM((2, 576, 768), BF16),
        pltpu.VMEM((2, 4, STACK, D), BF16),
        pltpu.VMEM((2, 4, WIN, STACK), BF16),
        pltpu.VMEM((2, 576, D), BF16),
        pltpu.VMEM((2, 576, D), F32),
        pltpu.VMEM((2, 576, 1), F32),
        pltpu.VMEM((2, 576, D), BF16),
        pltpu.VMEM((2, 576, 768), BF16),
        pltpu.VMEM((2, 576, 768), BF16),
        pltpu.VMEM((576, D), F32),
        pltpu.VMEM((576, D), F32),
        pltpu.VMEM((576, D), F32),
        pltpu.VMEM((HALO_ROWS, D), F32),
        pltpu.VMEM((HALO_ROWS, D), F32),
        pltpu.VMEM((4, HALO_ROWS, D), BF16),
        pltpu.VMEM((4, HALO_ROWS, D), BF16),
        pltpu.VMEM((576, D), BF16),
        pltpu.VMEM((576, 768), BF16),
        pltpu.VMEM((576, D), F32),
        pltpu.VMEM((576, D), BF16),
        pltpu.VMEM((576, D), BF16),
        pltpu.VMEM((STACK, D), BF16),
        pltpu.VMEM((WIN, STACK), BF16),
        pltpu.VMEM((576, 768), BF16),
        pltpu.VMEM((D, 768), F32),
        pltpu.VMEM((2, ROWS, 128), BF16),
        pltpu.VMEM((2, HALF, 128), BF16),
        pltpu.VMEM((2, HALF, 128), BF16),
        pltpu.VMEM((2, 16, PIECE, 128), BF16),
        pltpu.VMEM((2, 128, 128), BF16),
        pltpu.VMEM((2, 8, 16, 128), BF16),
        pltpu.VMEM((2, 128, 128), BF16),
        pltpu.VMEM((2, ROWS, 128), BF16),
        dma(4, 3), dma(4, 3),
        dma(2), dma(2),
        dma(2, 16), dma(2, 16),
        dma(2, 8), dma(2, 8),
        dma(2, 8), dma(2, 8),
        dma(2, 16), dma(2, 16),
        dma(2, 16), dma(2, 16),
        pltpu.SemaphoreType.DMA,
    ]
    res, gt, f = pl.pallas_call(
        megakernel,
        out_shape=(tile, tile, jax.ShapeDtypeStruct((2, ROWS, 128), BF16)),
        in_specs=[vmem] * 16,
        out_specs=(vmem, vmem, pl.BlockSpec(memory_space=pl.ANY)),
        scratch_shapes=scratch,
        compiler_params=pltpu.CompilerParams(
            collective_id=0, has_side_effects=True, vmem_limit_bytes=56 * 1024 * 1024
        ),
    )(
        tokens.reshape(24, 24, D), cotangent.reshape(24, 24, D),
        ga1, qkv1, proj1, gm1, up1, dn1, bias1.reshape(2, HEADS * WIN, WIN),
        ga2, qkv2, proj2, gm2, up2, dn2, bias2.reshape(2, HEADS * WIN, WIN),
    )
    one = [
        jax.ShapeDtypeStruct((D, 3 * D), F32),
        jax.ShapeDtypeStruct((D, D), F32),
        jax.ShapeDtypeStruct((D, 4 * D), F32),
        jax.ShapeDtypeStruct((4 * D, D), F32),
    ]
    outs = pl.pallas_call(
        functools.partial(unpack_kernel, 1.0 / math.sqrt(256.0 * 576.0)),
        out_shape=[tile, tile] + one + one,
        in_specs=[vmem] * 3,
        out_specs=[vmem] * 10,
        compiler_params=pltpu.CompilerParams(vmem_limit_bytes=48 * 1024 * 1024),
    )(f, res, gt)
    shape = (2, 12, 24, D)
    return (outs[0].reshape(shape), outs[1].reshape(shape)) + tuple(outs[2:])


def solution(mesh):
    grid = P(None, "lat", "lon", None)
    bias = P("lat", None, None, None, None)
    block = (P(), P(), P(), P(), P(), P(), bias)
    return jax.shard_map(
        body,
        mesh=mesh,
        in_specs=(grid,) + block + block + (grid,),
        out_specs=(grid, grid) + (P(),) * 8,
        check_vma=False,
    )
```

```python
import functools
import math

import jax
import jax.numpy as jnp
from jax import lax
from jax.experimental import pallas as pl
from jax.experimental.pallas import tpu as pltpu
from jax.sharding import PartitionSpec as P

F32 = jnp.float32
BF16 = jnp.bfloat16
HEADS = 6
WIN = 144
PAD = 11
D = 192
STACK = 896
SCALE = 32 ** -0.5
CHUNKS = ((0, 256), (256, 512), (512, 768), (768, 896))
PIECES = (112, 80, 48)
BASES = (0, 32 * 112, 32 * 192)
ROWS = 32 * 240
MESH = pl.DeviceIdType.MESH


def dot_nn(a, b):
    return lax.dot_general(a, b, (((1,), (0,)), ((), ())), preferred_element_type=F32)


def dot_nt(a, b):
    return lax.dot_general(a, b, (((1,), (1,)), ((), ())), preferred_element_type=F32)


def dot_tn(a, b):
    return lax.dot_general(a, b, (((0,), (0,)), ((), ())), preferred_element_type=F32)


def stage(name, work):
    work()


def win_rows(w):
    return pl.ds(pl.multiple_of(w * WIN, 16), WIN)


def normalise(x):
    mean = jnp.mean(x, axis=-1, keepdims=True)
    centred = x - mean
    var = jnp.mean(centred * centred, axis=-1, keepdims=True)
    r = lax.rsqrt(var + 1e-05)
    return centred * r, r


def normalise_back(dy, xhat, r):
    m1 = jnp.mean(dy, axis=-1, keepdims=True)
    m2 = jnp.mean(dy * xhat, axis=-1, keepdims=True)
    return r * (dy - m1 - xhat * m2)


def live_column(first_row, limit):
    n = lax.broadcasted_iota(jnp.int32, (WIN, 1), 0)
    m = jnp.where(n >= 72, n - 72, n)
    row = jnp.zeros_like(m)
    for i in range(1, 6):
        row = row + jnp.where(m >= 12 * i, 1, 0)
    pos = row + first_row
    return jnp.where((pos >= 0) & (pos < limit), 1.0, 0.0).astype(F32)


def head_mask(h, dtype):
    lane = lax.broadcasted_iota(jnp.int32, (1, D), 1)
    inside = (lane >= 32 * h) & (lane < 32 * h + 32)
    return jnp.where(inside, 1.0, 0.0).astype(F32).astype(dtype)


def tile_to_windows(src, dst):
    for level in range(2):
        for row in range(12):
            x = src[level * 12 + row].astype(F32)
            for wc in range(2):
                at = ((row // 6) * 2 + wc) * WIN + level * 72 + (row % 6) * 12
                dst[at : at + 12, :] = x[12 * wc : 12 * wc + 12, :]


def windows_to_tile(src, dst):
    for level in range(2):
        for row in range(12):
            parts = []
            for wc in range(2):
                at = ((row // 6) * 2 + wc) * WIN + level * 72 + (row % 6) * 12
                parts.append(src[at : at + 12, :])
            dst[level * 12 + row] = jnp.concatenate(parts, axis=0).astype(BF16)


def place(level, row, col):
    return ((row // 6) * 2 + col // 12) * WIN + level * 72 + (row % 6) * 12 + col % 12


def pack_halo(src, pack, out, row0, row1, col0, col1):
    at = 0
    for rows, cols in ((row0, col1), (row1, col0), (row1, col1)):
        for level in range(2):
            for row in rows:
                for col in cols:
                    p = place(level, row, col)
                    pack[at : at + 6, :] = src[p : p + 6, :]
                    at += 6
        at = (at + 15) // 16 * 16
    out[...] = pack[...].astype(BF16)


HALO_ROWS = 112 + 112 + 48
HALO_PARTS = ((0, 112), (112, 112), (224, 48))


def unpack_shift(src, halo, dst, step, windows):
    for level in range(2):
        for row in range(12):
            for col in range(0, 24, 6):
                if (row // 6) * 2 + col // 12 not in windows:
                    continue
                r, c = row - 3 * step, col - 6 * step
                r_in, c_in = 0 <= r < 12, 0 <= c < 24
                if r_in and c_in:
                    p = place(level, r, c)
                    piece = src[p : p + 6, :]
                else:
                    if r_in:
                        i = r if step > 0 else r - 3
                        at = (level * 9 + i) * 6
                    elif c_in:
                        i = row if step > 0 else row - 9
                        j = c if step > 0 else c - 6
                        at = 112 + (level * 3 + i) * 18 + j
                    else:
                        i = row if step > 0 else row - 9
                        at = 224 + (level * 3 + i) * 6
                    piece = halo[at : at + 6, :]
                q = place(level, row, col)
                dst[q : q + 6, :] = piece


def megakernel(
    tok, ct,
    ga1, qkv1, proj1, gm1, up1, dn1, bias1,
    ga2, qkv2, proj2, gm2, up2, dn2, bias2,
    res_o, gt_o, f_o,
    wp, bt, xhat1, r1, normed, proj_all, qm, pt, att, xhat2, r2, second, hidden, gp,
    cur, nxt, out2, cw, pack, halo_f, halo_out, halo_in,
    dtot, du, dres, dres_b, datt, dom, dst_, dqkv, w6,
    g_0, g_1, g_2, r_0, r_1, r_2, h_0, h_1, h_2, rr_0, rr_1, rr_2, z_0, z_1, z_2, f,
    halo_send, halo_recv, core_send, core_recv, xy_send, xy_recv, z_send, z_recv,
    ag_send, ag_recv, fw_send, fw_recv, out_sem,
):
    gs, r0s, hhs = (g_0, g_1, g_2), (r_0, r_1, r_2), (h_0, h_1, h_2)
    rrs, zs = (rr_0, rr_1, rr_2), (z_0, z_1, z_2)
    lon = lax.axis_index("lon")
    lat = lax.axis_index("lat")
    core = lax.rem(lon, 2)
    chip = lon // 2
    y_hi = lat // 8
    zi = lax.rem(lat, 8)
    me_xy = y_hi * 8 + chip

    def sibling():
        return {"lon": chip * 2 + 1 - core, "lat": lat}

    def xy_dev(j):
        return {"lon": lax.rem(j, 8) * 2 + core, "lat": (j // 8) * 8 + zi}

    def z_dev(j):
        return {"lon": lon, "lat": y_hi * 8 + j}

    def near(step_lon, step_lat):
        return {
            "lon": lax.rem(lon + step_lon + 16, 16),
            "lat": lax.rem(lat + step_lat + 16, 16),
        }

    barrier = pltpu.get_barrier_semaphore()

    def greet(device):
        pl.semaphore_signal(barrier, inc=1, device_id=device, device_id_type=MESH)

    greet(sibling())
    for k in range(1, 16):
        greet(xy_dev(lax.rem(me_xy + k, 16)))
    for k in range(1, 8):
        greet(z_dev(lax.rem(zi + k, 8)))
    for s in (1, -1):
        greet(near(s, 0))
        greet(near(0, s))
        greet(near(s, s))

    def halo_copy(x, part, step):
        first, count = HALO_PARTS[part]
        device = near(step if part != 1 else 0, step if part != 0 else 0)
        return pltpu.make_async_remote_copy(
            src_ref=halo_out.at[x, pl.ds(first, count)],
            dst_ref=halo_in.at[x, pl.ds(first, count)],
            send_sem=halo_send.at[x, part],
            recv_sem=halo_recv.at[x, part],
            device_id=device,
            device_id_type=MESH,
        )

    def halo_start(x, src, step):
        if step > 0:
            pack_halo(src, pack, halo_out.at[x], range(0, 9), range(9, 12), (0, 6, 12), (18,))
        else:
            pack_halo(src, pack, halo_out.at[x], range(3, 12), range(0, 3), (6, 12, 18), (0,))
        for part in range(3):
            halo_copy(x, part, step).start()

    def halo_finish(x, src, dst, step, windows=(0, 1, 2, 3)):
        for part in range(3):
            halo_copy(x, part, step).wait()
        outside = jnp.where(lat == (0 if step > 0 else 15), 0.0, 1.0).astype(F32)
        halo_f[0:112, :] = halo_in[x, 0:112].astype(F32)
        halo_f[112:, :] = halo_in[x, 112:].astype(F32) * outside
        unpack_shift(src, halo_f, dst, step, windows)

    limit = 16 * 12 - PAD
    starts = (lat * 12, lat * 12 - 3)
    weights = (
        (ga1, qkv1, proj1, gm1, up1, dn1, bias1),
        (ga2, qkv2, proj2, gm2, up2, dn2, bias2),
    )

    def live(b, w):
        return live_column(starts[b] + 6 * (w // 2), limit)

    def prepare(b):
        ga, wqkv, wproj, gm, wup, wdn, bias = weights[b]
        wp[b] = jnp.zeros((D, 768), BF16)
        for i in range(3):
            part = wqkv[...].astype(F32)[:, D * i : D * i + D]
            wp[b, :, 256 * i : 256 * i + D] = part.astype(BF16)
        rows_i = lax.broadcasted_iota(jnp.int32, (WIN, WIN), 0)
        cols_i = lax.broadcasted_iota(jnp.int32, (WIN, WIN), 1)
        eye = jnp.where(rows_i == cols_i, 1.0, 0.0).astype(F32).astype(BF16)
        for wr in range(2):
            penalty = (live_column(starts[b] + 6 * wr, limit) - 1.0) * 30000.0
            bt[wr, :, 0:864] = dot_nt(eye, bias[wr]) + penalty
            bt[wr, :, 864:] = jnp.zeros((WIN, STACK - 864), F32)

    def block_forward(b, x_in, x_out, lo, hi):
        ga, wqkv, wproj, gm, wup, wdn, bias = weights[b]
        gain_a = ga[...].reshape(1, D)
        gain_m = gm[...].reshape(1, D)

        def f_qkv(w):
            rows = win_rows(w)
            xh, r = normalise(x_in[rows, :])
            xhat1[b, rows, :] = xh
            r1[b, rows, :] = r
            nb = (xh * gain_a).astype(BF16)
            normed[b, rows, :] = nb
            proj_all[b, rows, :] = dot_nn(nb, wp[b]).astype(BF16)

        stage("f_qkv", lambda: pl.loop(lo, hi)(f_qkv))

        def f_att(w):
            rows = win_rows(w)
            wr = w // 2
            q = proj_all[b, rows, 0:D]
            k = proj_all[b, rows, 256 : 256 + D]
            v = proj_all[b, rows, 512 : 512 + D]
            for h in range(HEADS):
                qm[b, w, WIN * h : WIN * h + WIN, :] = q * head_mask(h, BF16)
            qm[b, w, 864:, :] = jnp.zeros((STACK - 864, D), BF16)
            for c0, c1 in CHUNKS:
                s = dot_nt(k, qm[b, w, c0:c1, :]) * SCALE + bt[wr, :, c0:c1]
                e = jnp.exp(s - jnp.max(s, axis=0, keepdims=True))
                total = jnp.sum(e, axis=0, keepdims=True)
                pt[b, w, :, c0:c1] = (e * (1.0 / total)).astype(BF16)
            o = dot_tn(pt[b, w], v)
            a = jnp.zeros((WIN, D), F32)
            for h in range(HEADS):
                a = a + o[WIN * h : WIN * h + WIN, :] * head_mask(h, F32)
            att[b, rows, :] = a.astype(BF16)

        stage("f_att", lambda: pl.loop(lo, hi)(f_att))

        def f_mlp(w):
            rows = win_rows(w)
            resid = x_in[rows, :] + dot_nn(att[b, rows, :], wproj[...])
            xh, r = normalise(resid)
            xhat2[b, rows, :] = xh
            r2[b, rows, :] = r
            sb = (xh * gain_m).astype(BF16)
            second[b, rows, :] = sb
            u = dot_nn(sb, wup[...])
            c = math.sqrt(2.0 / math.pi)
            u2 = u * u
            t = jnp.tanh(u * (c + (c * 0.044715) * u2))
            half = 0.5 + 0.5 * t
            hb = (u * half).astype(BF16)
            hidden[b, rows, :] = hb
            slope = half + u * (0.5 - 0.5 * t * t) * (c + (3 * c * 0.044715) * u2)
            gp[b, rows, :] = slope.astype(BF16)
            out = (resid + dot_nt(hb, wdn[...])) * live(b, w)
            x_out[rows, :] = out.astype(BF16).astype(F32)

        stage("f_mlp", lambda: pl.loop(lo, hi)(f_mlp))

    def mlp_backward(b, d_out, lo, hi):
        ga, wqkv, wproj, gm, wup, wdn, bias = weights[b]
        gain_m = gm[...].reshape(1, D)

        def b_mlp(w):
            rows = win_rows(w)
            dt = d_out[rows, :] * live(b, w)
            dtb = dt.astype(BF16)
            dtot[rows, :] = dtb
            dh = dot_nn(dtb, wdn[...]).astype(BF16).astype(F32)
            dub = (dh * gp[b, rows, :].astype(F32)).astype(BF16)
            du[rows, :] = dub
            dy = dot_nt(dub, wup[...]).astype(BF16).astype(F32) * gain_m
            dr = dt + normalise_back(dy, xhat2[b, rows, :], r2[b, rows, :])
            dres[rows, :] = dr
            drb = dr.astype(BF16)
            dres_b[rows, :] = drb
            datt[rows, :] = dot_nt(drb, wproj[...]).astype(BF16)

        stage("b_mlp", lambda: pl.loop(lo, hi)(b_mlp))

    def attention_backward(b, lo, hi, between=None):
        def b_att(w):
            rows = win_rows(w)
            k = proj_all[b, rows, 256 : 256 + D]
            v = proj_all[b, rows, 512 : 512 + D]
            do = datt[rows, :]
            for h in range(HEADS):
                dom[WIN * h : WIN * h + WIN, :] = do * head_mask(h, BF16)
            dom[864:, :] = jnp.zeros((STACK - 864, D), BF16)
            for c0, c1 in CHUNKS:
                dp = dot_nt(v, dom[c0:c1, :]).astype(BF16).astype(F32)
                p = pt[b, w, :, c0:c1].astype(F32)
                delta = jnp.sum(p * dp, axis=0, keepdims=True)
                dst_[:, c0:c1] = (p * (dp - delta)).astype(BF16)
            zeros = jnp.zeros((WIN, 64), BF16)
            dqkv[rows, 512 : 512 + D] = dot_nn(pt[b, w], dom[...]).astype(BF16)
            dqkv[rows, 256 : 256 + D] = (dot_nn(dst_[...], qm[b, w]) * SCALE).astype(BF16)
            o = dot_tn(dst_[...], k)
            a = jnp.zeros((WIN, D), F32)
            for h in range(HEADS):
                a = a + o[WIN * h : WIN * h + WIN, :] * head_mask(h, F32)
            dqkv[rows, 0:D] = (a * SCALE).astype(BF16)
            for i in range(3):
                dqkv[rows, 256 * i + D : 256 * i + 256] = zeros

            if between is not None:
                between(w)

        stage("b_att", lambda: pl.loop(lo, hi)(b_att))

    def input_backward(b, d_in, lo, hi):
        gain_a = weights[b][0][...].reshape(1, D)

        def b_qkv(w):
            rows = win_rows(w)
            dy = dot_nt(dqkv[rows, :], wp[b]).astype(BF16).astype(F32) * gain_a
            dx = dres[rows, :] + normalise_back(dy, xhat1[b, rows, :], r1[b, rows, :])
            d_in[rows, :] = dx.astype(BF16).astype(F32)

        stage("b_qkv", lambda: pl.loop(lo, hi)(b_qkv))

    def put(gr, at, matrix):
        for i in range(6):
            gs[gr][at + i * D : at + i * D + D, :] = matrix[:, 128 * i : 128 * i + 128].astype(BF16)

    def mlp_terms(b, gr, at):
        put(gr, at, dot_tn(second[b], du[...]))
        put(gr, at + 6 * D, dot_tn(dtot[...], hidden[b]))

    def attention_terms(b, gr, at):
        w6[...] = dot_tn(normed[b], dqkv[...])
        pr = dot_tn(att[b], dres_b[...])
        for i in range(3):
            w6[:, 256 * i + D : 256 * i + 256] = pr[:, 64 * i : 64 * i + 64]
        put(gr, at, w6)

    def remote(src, dst, send, recv, device):
        return pltpu.make_async_remote_copy(
            src_ref=src, dst_ref=dst, send_sem=send, recv_sem=recv,
            device_id=device, device_id_type=MESH,
        )

    def piece_at(gr, j):
        return pl.ds(pl.multiple_of(j * PIECES[gr], 16), PIECES[gr])

    def f_at(gr, c, j):
        return pl.ds(pl.multiple_of(BASES[gr] + (c * 16 + j) * PIECES[gr], 16), PIECES[gr])

    def core_copy(gr):
        rows = 16 * PIECES[gr]
        there = pl.ds(pl.multiple_of((1 - core) * rows, 16), rows)
        return remote(gs[gr].at[there], r0s[gr], core_send.at[gr], core_recv.at[gr], sibling())

    def xy_copy(gr, j, slot):
        return remote(
            hhs[gr].at[piece_at(gr, j)], rrs[gr].at[slot],
            xy_send.at[gr, j], xy_recv.at[gr, slot], xy_dev(j),
        )

    def z_copy(gr, j, slot):
        return remote(zs[gr].at[slot], zs[gr].at[slot], z_send.at[gr, j], z_recv.at[gr, slot], z_dev(j))

    def ag_copy(gr, j, slot):
        at = f_at(gr, core, slot)
        return remote(f.at[at], f.at[at], ag_send.at[gr, j], ag_recv.at[gr, slot], xy_dev(j))

    def fw_copy(gr, j, c):
        at = f_at(gr, c, j)
        return remote(f.at[at], f.at[at], fw_send.at[gr, j], fw_recv.at[gr, j], sibling())

    def xy_others(body):
        def step(k, carry):
            body(lax.rem(me_xy + k, 16))
            return carry
        lax.fori_loop(1, 16, step, 0)

    def z_others(body):
        def step(k, carry):
            body(lax.rem(zi + k, 8))
            return carry
        lax.fori_loop(1, 8, step, 0)

    def sum_0(gr):
        core_copy(gr).start()

    def sum_1(gr):
        core_copy(gr).wait()

        def add(j):
            own = gs[gr][pl.ds(pl.multiple_of((core * 16 + j) * PIECES[gr], 16), PIECES[gr]), :]
            there = r0s[gr][piece_at(gr, j), :]
            hhs[gr][piece_at(gr, j), :] = (own.astype(F32) + there.astype(F32)).astype(BF16)

        def add_and_send(j):
            add(j)
            xy_copy(gr, j, me_xy).start()

        xy_others(add_and_send)
        add(me_xy)

    def sum_2(gr):
        def step(k, total):
            j = lax.rem(me_xy + k, 16)
            xy_copy(gr, me_xy, j).wait_recv()
            return total + rrs[gr][j].astype(F32)

        own = hhs[gr][piece_at(gr, me_xy), :].astype(F32)
        zs[gr][zi] = lax.fori_loop(1, 16, step, own).astype(BF16)
        z_others(lambda j: z_copy(gr, j, zi).start())

    def sum_3(gr):
        z_others(lambda j: z_copy(gr, zi, j).wait_recv())
        total = zs[gr][0].astype(F32)
        for j in range(1, 8):
            total = total + zs[gr][j].astype(F32)
        f[f_at(gr, core, me_xy), :] = total.astype(BF16)
        xy_others(lambda j: ag_copy(gr, j, me_xy).start())
        fw_copy(gr, me_xy, core).start()

    def sum_4(gr):
        def forward(j):
            ag_copy(gr, me_xy, j).wait_recv()
            fw_copy(gr, j, core).start()
        xy_others(forward)

    def sum_5(gr):
        def arrived(j, carry):
            fw_copy(gr, j, 1 - core).wait_recv()
            fw_copy(gr, j, core).wait_send()
            return carry
        lax.fori_loop(0, 16, arrived, 0)

    def sum_sent(gr):
        def sent(j):
            xy_copy(gr, j, me_xy).wait_send()
            ag_copy(gr, j, me_xy).wait_send()
        xy_others(sent)
        z_others(lambda j: z_copy(gr, j, zi).wait_send())

    def out_copy(gr):
        at = pl.ds(BASES[gr], 32 * PIECES[gr])
        return pltpu.make_async_copy(f.at[at], f_o.at[at], out_sem.at[gr])

    def aside(w):
        @pl.when(w == 1)
        def _():
            sum_1(1)

        @pl.when(w == 3)
        def _():
            sum_2(0)

    for gr in range(3):
        used = (18, 12, 6)[gr] * D
        gs[gr][used:, :] = jnp.zeros((32 * PIECES[gr] - used, 128), BF16)
    tile_to_windows(tok, cur)
    tile_to_windows(ct, cw)
    prepare(0)
    pl.semaphore_wait(barrier, 29)
    halo_start(0, cw, 1)
    block_forward(0, cur, nxt, 1, 4)
    halo_start(1, nxt, 1)
    block_forward(0, cur, nxt, 0, 1)
    prepare(1)
    unpack_shift(nxt, halo_f, cur, 1, (3,))
    block_forward(1, cur, out2, 3, 4)
    halo_finish(1, nxt, cur, 1, (0, 1, 2))
    block_forward(1, cur, out2, 0, 3)
    halo_start(2, out2, -1)
    halo_finish(0, cw, cur, 1)
    mlp_backward(1, cur, 0, 3)
    attention_backward(1, 0, 3)
    input_backward(1, cw, 0, 3)
    halo_start(3, cw, -1)
    mlp_backward(1, cur, 3, 4)
    attention_backward(1, 3, 4)
    input_backward(1, cw, 3, 4)
    mlp_terms(1, 0, 6 * D)
    attention_terms(1, 0, 0)
    sum_0(0)
    unpack_shift(cw, halo_f, nxt, -1, (0,))
    mlp_backward(0, nxt, 0, 1)
    sum_1(0)
    halo_finish(3, cw, nxt, -1, (1, 2, 3))
    mlp_backward(0, nxt, 1, 4)
    mlp_terms(0, 1, 0)
    sum_0(1)
    attention_backward(0, 0, 4, aside)
    attention_terms(0, 2, 0)
    sum_0(2)
    input_backward(0, cur, 0, 4)
    sum_1(2)
    windows_to_tile(cur, gt_o)
    halo_finish(2, out2, nxt, -1)
    windows_to_tile(nxt, res_o)
    sum_2(1)
    sum_3(0)
    sum_2(2)
    sum_3(1)
    sum_4(0)
    sum_3(2)
    sum_4(1)
    sum_4(2)
    for gr in range(3):
        sum_5(gr)
        out_copy(gr).start()
    for gr in range(3):
        sum_sent(gr)
        out_copy(gr).wait()


def unpack_kernel(factor, f_in, res, gt, res_o, gt_o, *refs):
    outs, f, held, sems = refs[:8], refs[8], refs[9:17], refs[17]
    res_v, gt_v = refs[18], refs[19]
    copies = []
    fields = [
        pltpu.make_async_copy(res, res_v, sems.at[0]),
        pltpu.make_async_copy(gt, gt_v, sems.at[1]),
    ]
    parts = [
        pltpu.make_async_copy(f_in.at[at], f.at[at], sems.at[2 + i])
        for i, at in enumerate(
            pl.ds(BASES[gr], 32 * PIECES[gr]) for gr in range(3)
        )
    ]
    for copy in parts + fields:
        copy.start()

    def tile(gr, i):
        at = BASES[gr] + i * D
        return f[at : at + D, :].astype(F32) * factor

    def attention_out(gr, i, qkv, proj):
        for n in range(3):
            two = jnp.concatenate([tile(gr, i + 2 * n), tile(gr, i + 2 * n + 1)], axis=1)
            qkv[:, D * n : D * n + D] = two[:, 0:D]
            proj[:, 64 * n : 64 * n + 64] = two[:, D:]

    def mlp_out(gr, i, up, down):
        for n in range(6):
            up[:, 128 * n : 128 * n + 128] = tile(gr, i + n)
            down[:, 128 * n : 128 * n + 128] = tile(gr, i + 6 + n)

    def send(first, count):
        for i in range(first, first + count):
            copy = pltpu.make_async_copy(held[i], outs[i], sems.at[5 + i])
            copy.start()
            copies.append(copy)

    parts[0].wait()
    mlp_out(0, 6, held[6], held[7])
    send(6, 2)
    attention_out(0, 0, held[4], held[5])
    send(4, 2)
    for i, (held_f, out_f) in enumerate(((res_v, res_o), (gt_v, gt_o))):
        fields[i].wait()
        copy = pltpu.make_async_copy(held_f, out_f, sems.at[i])
        copy.start()
        copies.append(copy)
    parts[1].wait()
    mlp_out(1, 0, held[2], held[3])
    send(2, 2)
    parts[2].wait()
    attention_out(2, 0, held[0], held[1])
    send(0, 2)
    for copy in copies:
        copy.wait()


def body(
    tokens, ga1, qkv1, proj1, gm1, up1, dn1, bias1,
    ga2, qkv2, proj2, gm2, up2, dn2, bias2, cotangent,
):
    vmem = pl.BlockSpec(memory_space=pltpu.VMEM)
    tile = jax.ShapeDtypeStruct((24, 24, D), BF16)

    def dma(*shape):
        return pltpu.SemaphoreType.DMA(shape)

    scratch = [
        pltpu.VMEM((2, D, 768), BF16),
        pltpu.VMEM((2, WIN, STACK), F32),
        pltpu.VMEM((2, 576, D), F32),
        pltpu.VMEM((2, 576, 1), F32),
        pltpu.VMEM((2, 576, D), BF16),
        pltpu.VMEM((2, 576, 768), BF16),
        pltpu.VMEM((2, 4, STACK, D), BF16),
        pltpu.VMEM((2, 4, WIN, STACK), BF16),
        pltpu.VMEM((2, 576, D), BF16),
        pltpu.VMEM((2, 576, D), F32),
        pltpu.VMEM((2, 576, 1), F32),
        pltpu.VMEM((2, 576, D), BF16),
        pltpu.VMEM((2, 576, 768), BF16),
        pltpu.VMEM((2, 576, 768), BF16),
        pltpu.VMEM((576, D), F32),
        pltpu.VMEM((576, D), F32),
        pltpu.VMEM((576, D), F32),
        pltpu.VMEM((576, D), F32),
        pltpu.VMEM((HALO_ROWS, D), F32),
        pltpu.VMEM((HALO_ROWS, D), F32),
        pltpu.VMEM((4, HALO_ROWS, D), BF16),
        pltpu.VMEM((4, HALO_ROWS, D), BF16),
        pltpu.VMEM((576, D), BF16),
        pltpu.VMEM((576, 768), BF16),
        pltpu.VMEM((576, D), F32),
        pltpu.VMEM((576, D), BF16),
        pltpu.VMEM((576, D), BF16),
        pltpu.VMEM((STACK, D), BF16),
        pltpu.VMEM((WIN, STACK), BF16),
        pltpu.VMEM((576, 768), BF16),
        pltpu.VMEM((D, 768), F32),
        *[pltpu.VMEM((32 * r, 128), BF16) for r in PIECES],
        *[pltpu.VMEM((16 * r, 128), BF16) for r in PIECES],
        *[pltpu.VMEM((16 * r, 128), BF16) for r in PIECES],
        *[pltpu.VMEM((16, r, 128), BF16) for r in PIECES],
        *[pltpu.VMEM((8, r, 128), BF16) for r in PIECES],
        pltpu.VMEM((ROWS, 128), BF16),
        dma(4, 3), dma(4, 3),
        dma(3), dma(3),
        dma(3, 16), dma(3, 16),
        dma(3, 8), dma(3, 8),
        dma(3, 16), dma(3, 16),
        dma(3, 16), dma(3, 16),
        dma(3),
    ]
    res, gt, f = pl.pallas_call(
        megakernel,
        out_shape=(tile, tile, jax.ShapeDtypeStruct((ROWS, 128), BF16)),
        in_specs=[vmem] * 16,
        out_specs=(vmem, vmem, pl.BlockSpec(memory_space=pl.ANY)),
        scratch_shapes=scratch,
        compiler_params=pltpu.CompilerParams(
            collective_id=0, has_side_effects=True, vmem_limit_bytes=56 * 1024 * 1024
        ),
    )(
        tokens.reshape(24, 24, D), cotangent.reshape(24, 24, D),
        ga1, qkv1, proj1, gm1, up1, dn1.T, bias1.reshape(2, HEADS * WIN, WIN),
        ga2, qkv2, proj2, gm2, up2, dn2.T, bias2.reshape(2, HEADS * WIN, WIN),
    )
    one = [
        jax.ShapeDtypeStruct((D, 3 * D), F32),
        jax.ShapeDtypeStruct((D, D), F32),
        jax.ShapeDtypeStruct((D, 4 * D), F32),
        jax.ShapeDtypeStruct((D, 4 * D), F32),
    ]
    anywhere = pl.BlockSpec(memory_space=pl.ANY)
    outs = list(pl.pallas_call(
        functools.partial(unpack_kernel, 1.0 / math.sqrt(256.0 * 576.0)),
        out_shape=[tile, tile] + one + one,
        in_specs=[anywhere] * 3,
        out_specs=[anywhere] * 10,
        scratch_shapes=[pltpu.VMEM((ROWS, 128), BF16)]
        + [pltpu.VMEM(s.shape, F32) for s in one + one]
        + [dma(13), pltpu.VMEM(tile.shape, BF16), pltpu.VMEM(tile.shape, BF16)],
        compiler_params=pltpu.CompilerParams(vmem_limit_bytes=60 * 1024 * 1024),
    )(f, res, gt))
    shape = (2, 12, 24, D)
    terms = outs[2:5] + [outs[5].T] + outs[6:9] + [outs[9].T]
    return (outs[0].reshape(shape), outs[1].reshape(shape)) + tuple(terms)


def solution(mesh):
    grid = P(None, "lat", "lon", None)
    bias = P("lat", None, None, None, None)
    block = (P(), P(), P(), P(), P(), P(), bias)
    return jax.shard_map(
        body,
        mesh=mesh,
        in_specs=(grid,) + block + block + (grid,),
        out_specs=(grid, grid) + (P(),) * 8,
        check_vma=False,
    )
```

```python
import functools
import math

import jax
import jax.numpy as jnp
from jax import lax
from jax.experimental import pallas as pl
from jax.experimental.pallas import tpu as pltpu
from jax.sharding import PartitionSpec as P

F32 = jnp.float32
BF16 = jnp.bfloat16
HEADS = 6
WIN = 144
PAD = 11
D = 192
STACK = 896
SCALE = 32 ** -0.5
CHUNKS = ((0, 256), (256, 512), (512, 768), (768, 896))
PIECES = (80, 48, 80, 48)
BASES = (0, 32 * 80, 32 * 128, 32 * 208)
ROWS = 32 * 256
GROUPS = 4
MESH = pl.DeviceIdType.MESH


def dot_nn(a, b):
    return lax.dot_general(a, b, (((1,), (0,)), ((), ())), preferred_element_type=F32)


def dot_nt(a, b):
    return lax.dot_general(a, b, (((1,), (1,)), ((), ())), preferred_element_type=F32)


def dot_tn(a, b):
    return lax.dot_general(a, b, (((0,), (0,)), ((), ())), preferred_element_type=F32)


def stage(name, work):
    work()


def win_rows(w):
    return pl.ds(pl.multiple_of(w * WIN, 16), WIN)


def lane_mean(x):
    return dot_nn(x, jnp.ones((D, D), BF16)) * (1.0 / D)


def normalise(x, exact):
    high = x.astype(BF16)
    mean = lane_mean(high)
    if not exact:
        mean = mean + lane_mean((x - high.astype(F32)).astype(BF16))
    centred = x - mean
    r = lax.rsqrt(lane_mean((centred * centred).astype(BF16)) + 1e-05)
    return centred * r, r


def normalise_back(dy, xhat, r):
    m1 = lane_mean(dy.astype(BF16))
    m2 = lane_mean((dy * xhat).astype(BF16))
    return r * (dy - m1 - xhat * m2)


def live_column(first_row, limit):
    n = lax.broadcasted_iota(jnp.int32, (WIN, 1), 0)
    m = jnp.where(n >= 72, n - 72, n)
    row = jnp.zeros_like(m)
    for i in range(1, 6):
        row = row + jnp.where(m >= 12 * i, 1, 0)
    pos = row + first_row
    return jnp.where((pos >= 0) & (pos < limit), 1.0, 0.0).astype(F32)


def head_mask(h, dtype):
    lane = lax.broadcasted_iota(jnp.int32, (1, D), 1)
    inside = (lane >= 32 * h) & (lane < 32 * h + 32)
    return jnp.where(inside, 1.0, 0.0).astype(F32).astype(dtype)


def own_lanes(o):
    lane = lax.broadcasted_iota(jnp.int32, (1, 128), 1)
    left = o[3 * WIN : 4 * WIN, 0:128]
    for h in (2, 1, 0):
        left = jnp.where(lane < 32 * h + 32, o[WIN * h : WIN * h + WIN, 0:128], left)
    right = jnp.where(
        lane[:, 0:64] < 32, o[4 * WIN : 5 * WIN, 128:D], o[5 * WIN : 6 * WIN, 128:D]
    )
    return jnp.concatenate([left, right], axis=1)


def tile_to_windows(src, dst):
    for level in range(2):
        for row in range(12):
            x = src[level * 12 + row].astype(F32)
            for wc in range(2):
                at = ((row // 6) * 2 + wc) * WIN + level * 72 + (row % 6) * 12
                dst[at : at + 12, :] = x[12 * wc : 12 * wc + 12, :]


def windows_to_tile(src, dst):
    for level in range(2):
        for row in range(12):
            parts = []
            for wc in range(2):
                at = ((row // 6) * 2 + wc) * WIN + level * 72 + (row % 6) * 12
                parts.append(src[at : at + 12, :])
            dst[level * 12 + row] = jnp.concatenate(parts, axis=0).astype(BF16)


def place(level, row, col):
    return ((row // 6) * 2 + col // 12) * WIN + level * 72 + (row % 6) * 12 + col % 12


def pack_halo(src, pack, out, row0, row1, col0, col1):
    at = 0
    for rows, cols in ((row0, col1), (row1, col0), (row1, col1)):
        for level in range(2):
            for row in rows:
                for col in cols:
                    p = place(level, row, col)
                    pack[at : at + 6, :] = src[p : p + 6, :]
                    at += 6
        at = (at + 15) // 16 * 16
    out[...] = pack[...].astype(BF16)


HALO_ROWS = 112 + 112 + 48
HALO_PARTS = ((0, 112), (112, 112), (224, 48))


def unpack_shift(src, halo, dst, step, windows):
    for level in range(2):
        for row in range(12):
            for col in range(0, 24, 6):
                if (row // 6) * 2 + col // 12 not in windows:
                    continue
                r, c = row - 3 * step, col - 6 * step
                r_in, c_in = 0 <= r < 12, 0 <= c < 24
                if r_in and c_in:
                    p = place(level, r, c)
                    piece = src[p : p + 6, :]
                else:
                    if r_in:
                        i = r if step > 0 else r - 3
                        at = (level * 9 + i) * 6
                    elif c_in:
                        i = row if step > 0 else row - 9
                        j = c if step > 0 else c - 6
                        at = 112 + (level * 3 + i) * 18 + j
                    else:
                        i = row if step > 0 else row - 9
                        at = 224 + (level * 3 + i) * 6
                    piece = halo[at : at + 6, :]
                q = place(level, row, col)
                dst[q : q + 6, :] = piece


def megakernel(
    ga1, gm1, ga2, gm2, tok, ct, qkv1, proj1, up1, dn1, bias1, qkv2, proj2, up2, dn2, bias2,
    res_o, gt_o, f_o,
    wp, bt, alive, xhat1, r1, normed, proj_all, qm, pt, att, xhat2, r2, second, hidden, gp,
    res_v, gt_v, f, cur, nxt, out2, cw, pack, halo_f, halo_out, halo_in,
    dtot, du, dres, dres_b, datt, dom, dst_, dqkv, w6, *refs
):
    gs, r0s, hhs, rrs, zs = (refs[GROUPS * i : GROUPS * i + GROUPS] for i in range(5))
    held, sems = refs[5 * GROUPS : 5 * GROUPS + 12], refs[5 * GROUPS + 12 :]
    (
        halo_send, halo_recv, core_send, core_recv, xy_send, xy_recv, z_send, z_recv,
        ag_send, ag_recv, fw_send, fw_recv, out_sem, in_sem,
    ) = sems
    loads = [
        pltpu.make_async_copy(there, here, in_sem.at[i])
        for i, (there, here) in enumerate(
            zip((tok, ct, qkv1, proj1, up1, dn1, bias1, qkv2, proj2, up2, dn2, bias2), held)
        )
    ]
    for i in (0, 2, 6, 1, 3, 4, 5, 7, 11, 8, 9, 10):
        loads[i].start()
    tok, ct, qkv1, proj1, up1, dn1, bias1, qkv2, proj2, up2, dn2, bias2 = held
    lon = lax.axis_index("lon")
    lat = lax.axis_index("lat")
    core = lax.rem(lon, 2)
    chip = lon // 2
    y_hi = lat // 8
    zi = lax.rem(lat, 8)
    me_xy = y_hi * 8 + chip

    def sibling():
        return {"lon": chip * 2 + 1 - core, "lat": lat}

    def xy_dev(j):
        return {"lon": lax.rem(j, 8) * 2 + core, "lat": (j // 8) * 8 + zi}

    def z_dev(j):
        return {"lon": lon, "lat": y_hi * 8 + j}

    def near(step_lon, step_lat):
        return {
            "lon": lax.rem(lon + step_lon + 16, 16),
            "lat": lax.rem(lat + step_lat + 16, 16),
        }

    barrier = pltpu.get_barrier_semaphore()

    def greet(device):
        pl.semaphore_signal(barrier, inc=1, device_id=device, device_id_type=MESH)

    greet(sibling())
    for k in range(1, 16):
        greet(xy_dev(lax.rem(me_xy + k, 16)))
    for k in range(1, 8):
        greet(z_dev(lax.rem(zi + k, 8)))
    for s in (1, -1):
        greet(near(s, 0))
        greet(near(0, s))
        greet(near(s, s))

    def halo_copy(x, part, step):
        first, count = HALO_PARTS[part]
        device = near(step if part != 1 else 0, step if part != 0 else 0)
        return pltpu.make_async_remote_copy(
            src_ref=halo_out.at[x, pl.ds(first, count)],
            dst_ref=halo_in.at[x, pl.ds(first, count)],
            send_sem=halo_send.at[x, part],
            recv_sem=halo_recv.at[x, part],
            device_id=device,
            device_id_type=MESH,
        )

    def halo_start(x, src, step):
        if step > 0:
            pack_halo(src, pack, halo_out.at[x], range(0, 9), range(9, 12), (0, 6, 12), (18,))
        else:
            pack_halo(src, pack, halo_out.at[x], range(3, 12), range(0, 3), (6, 12, 18), (0,))
        for part in range(3):
            halo_copy(x, part, step).start()

    def halo_finish(x, src, dst, step, windows=(0, 1, 2, 3)):
        for part in range(3):
            halo_copy(x, part, step).wait()
        outside = jnp.where(lat == (0 if step > 0 else 15), 0.0, 1.0).astype(F32)
        halo_f[0:112, :] = halo_in[x, 0:112].astype(F32)
        halo_f[112:, :] = halo_in[x, 112:].astype(F32) * outside
        unpack_shift(src, halo_f, dst, step, windows)

    limit = 16 * 12 - PAD
    starts = (lat * 12, lat * 12 - 3)
    weights = (
        (ga1, qkv1, proj1, gm1, up1, dn1, bias1),
        (ga2, qkv2, proj2, gm2, up2, dn2, bias2),
    )

    def prepare(b):
        ga, wqkv, wproj, gm, wup, wdn, bias = weights[b]
        wp[b] = jnp.zeros((D, 768), BF16)
        for i in range(3):
            part = wqkv[...].astype(F32)[:, D * i : D * i + D]
            wp[b, :, 256 * i : 256 * i + D] = part.astype(BF16)
        rows_i = lax.broadcasted_iota(jnp.int32, (WIN, WIN), 0)
        cols_i = lax.broadcasted_iota(jnp.int32, (WIN, WIN), 1)
        eye = jnp.where(rows_i == cols_i, 1.0, 0.0).astype(F32).astype(BF16)
        for wr in range(2):
            here = live_column(starts[b] + 6 * wr, limit)
            penalty = (here - 1.0) * 30000.0
            for wc in range(2):
                alive[b, (2 * wr + wc) * WIN : (2 * wr + wc + 1) * WIN, :] = here
            bt[wr, :, 0:864] = dot_nt(eye, bias[wr]) + penalty
            bt[wr, :, 864:] = jnp.zeros((WIN, STACK - 864), F32)

    def block_forward(b, x_in, x_out, lo, hi):
        ga, wqkv, wproj, gm, wup, wdn, bias = weights[b]
        gain_a = ga[...].reshape(1, D)
        gain_m = gm[...].reshape(1, D)

        span = slice(lo * WIN, hi * WIN)

        def f_qkv():
            xh, r = normalise(x_in[span, :], True)
            xhat1[b, span, :] = xh
            r1[b, span, :] = r
            normed[b, span, :] = (xh * gain_a).astype(BF16)
            proj_all[b, span, :] = dot_nn(normed[b, span, :], wp[b]).astype(BF16)

        stage("f_qkv", f_qkv)

        def f_att(w):
            rows = win_rows(w)
            wr = w // 2
            q = proj_all[b, rows, 0:D]
            k = proj_all[b, rows, 256 : 256 + D]
            v = proj_all[b, rows, 512 : 512 + D]
            for h in range(HEADS):
                qm[b, w, WIN * h : WIN * h + WIN, :] = q * head_mask(h, BF16)
            qm[b, w, 864:, :] = jnp.zeros((STACK - 864, D), BF16)
            for c0, c1 in CHUNKS:
                s = dot_nt(k, qm[b, w, c0:c1, :]) * SCALE + bt[wr, :, c0:c1]
                e = jnp.exp(s - jnp.max(s, axis=0, keepdims=True))
                total = jnp.sum(e, axis=0, keepdims=True)
                pt[b, w, :, c0:c1] = (e * (1.0 / total)).astype(BF16)
            o = dot_tn(pt[b, w], v)
            a = own_lanes(o)
            att[b, rows, :] = a.astype(BF16)

        stage("f_att", lambda: [f_att(w) for w in range(lo, hi)])

        def f_mlp():
            resid = x_in[span, :] + dot_nn(att[b, span, :], wproj[...])
            x_out[span, :] = resid
            xh, r = normalise(resid, False)
            xhat2[b, span, :] = xh
            r2[b, span, :] = r
            second[b, span, :] = (xh * gain_m).astype(BF16)
            c = math.sqrt(2.0 / math.pi)
            for n in range(3):
                at = slice(256 * n, 256 * n + 256)
                u = dot_nn(second[b, span, :], wup[:, at])
                u2 = u * u
                t = jnp.tanh(u * (c + (c * 0.044715) * u2))
                half = 0.5 + 0.5 * t
                hidden[b, span, at] = (u * half).astype(BF16)
                slope = half + u * (half * (1.0 - half)) * (2 * c + (6 * c * 0.044715) * u2)
                gp[b, span, at] = slope.astype(BF16)
            out = (x_out[span, :] + dot_nt(hidden[b, span, :], wdn[...])) * alive[b, span, :]
            x_out[span, :] = out.astype(BF16).astype(F32)

        stage("f_mlp", f_mlp)

    def mlp_backward(b, d_out, lo, hi):
        ga, wqkv, wproj, gm, wup, wdn, bias = weights[b]
        gain_m = gm[...].reshape(1, D)

        span = slice(lo * WIN, hi * WIN)

        def b_mlp():
            dtb = (d_out[span, :] * alive[b, span, :]).astype(BF16)
            dtot[span, :] = dtb
            for n in range(3):
                at = slice(256 * n, 256 * n + 256)
                dh = dot_nn(dtot[span, :], wdn[:, at]).astype(BF16).astype(F32)
                du[span, at] = (dh * gp[b, span, at].astype(F32)).astype(BF16)
            dy = dot_nt(du[span, :], wup[...]).astype(BF16).astype(F32) * gain_m
            dr = dtot[span, :].astype(F32) + normalise_back(dy, xhat2[b, span, :], r2[b, span, :])
            dres[span, :] = dr
            dres_b[span, :] = dr.astype(BF16)
            datt[span, :] = dot_nt(dres_b[span, :], wproj[...]).astype(BF16)

        stage("b_mlp", b_mlp)

    def attention_backward(b, lo, hi, between=None):
        def b_att(w):
            rows = win_rows(w)
            k = proj_all[b, rows, 256 : 256 + D]
            v = proj_all[b, rows, 512 : 512 + D]
            do = datt[rows, :]
            for h in range(HEADS):
                dom[w, WIN * h : WIN * h + WIN, :] = do * head_mask(h, BF16)
            dom[w, 864:, :] = jnp.zeros((STACK - 864, D), BF16)
            for c0, c1 in CHUNKS:
                dp = dot_nt(v, dom[w, c0:c1, :]).astype(BF16).astype(F32)
                p = pt[b, w, :, c0:c1].astype(F32)
                delta = jnp.sum(p * dp, axis=0, keepdims=True)
                dst_[w, :, c0:c1] = (p * (dp - delta)).astype(BF16)
            zeros = jnp.zeros((WIN, 64), BF16)
            dqkv[rows, 512 : 512 + D] = dot_nn(pt[b, w], dom[w]).astype(BF16)
            dqkv[rows, 256 : 256 + D] = (dot_nn(dst_[w], qm[b, w]) * SCALE).astype(BF16)
            o = dot_tn(dst_[w], k)
            a = own_lanes(o)
            dqkv[rows, 0:D] = (a * SCALE).astype(BF16)
            for i in range(3):
                dqkv[rows, 256 * i + D : 256 * i + 256] = zeros

            if between is not None:
                between(w)

        stage("b_att", lambda: [b_att(w) for w in range(lo, hi)])

    def input_backward(b, d_in, lo, hi):
        gain_a = weights[b][0][...].reshape(1, D)

        span = slice(lo * WIN, hi * WIN)

        def b_qkv():
            dy = dot_nt(dqkv[span, :], wp[b]).astype(BF16).astype(F32) * gain_a
            dx = dres[span, :] + normalise_back(dy, xhat1[b, span, :], r1[b, span, :])
            d_in[span, :] = dx.astype(BF16).astype(F32)

        stage("b_qkv", b_qkv)

    def put(gr, at, matrix):
        for i in range(6):
            gs[gr][at + i * D : at + i * D + D, :] = matrix[:, 128 * i : 128 * i + 128].astype(BF16)

    def mlp_terms(b, gr, at):
        put(gr, at, dot_tn(second[b], du[...]))
        put(gr, at + 6 * D, dot_tn(dtot[...], hidden[b]))

    def attention_terms(b, gr, at):
        w6[...] = dot_tn(normed[b], dqkv[...])
        pr = dot_tn(att[b], dres_b[...])
        for i in range(3):
            w6[:, 256 * i + D : 256 * i + 256] = pr[:, 64 * i : 64 * i + 64]
        put(gr, at, w6)

    def remote(src, dst, send, recv, device):
        return pltpu.make_async_remote_copy(
            src_ref=src, dst_ref=dst, send_sem=send, recv_sem=recv,
            device_id=device, device_id_type=MESH,
        )

    def piece_at(gr, j):
        return pl.ds(pl.multiple_of(j * PIECES[gr], 16), PIECES[gr])

    def f_at(gr, c, j):
        return pl.ds(pl.multiple_of(BASES[gr] + (c * 16 + j) * PIECES[gr], 16), PIECES[gr])

    def core_copy(gr):
        rows = 16 * PIECES[gr]
        there = pl.ds(pl.multiple_of((1 - core) * rows, 16), rows)
        return remote(gs[gr].at[there], r0s[gr], core_send.at[gr], core_recv.at[gr], sibling())

    def xy_copy(gr, j, slot):
        return remote(
            hhs[gr].at[piece_at(gr, j)], rrs[gr].at[slot],
            xy_send.at[gr, j], xy_recv.at[gr, slot], xy_dev(j),
        )

    def z_copy(gr, j, slot):
        return remote(zs[gr].at[slot], zs[gr].at[slot], z_send.at[gr, j], z_recv.at[gr, slot], z_dev(j))

    def ag_copy(gr, j, slot):
        at = f_at(gr, core, slot)
        return remote(f.at[at], f.at[at], ag_send.at[gr, j], ag_recv.at[gr, slot], xy_dev(j))

    def fw_copy(gr, j, c):
        at = f_at(gr, c, j)
        return remote(f.at[at], f.at[at], fw_send.at[gr, j], fw_recv.at[gr, j], sibling())

    def xy_others(body):
        def step(k, carry):
            body(lax.rem(me_xy + k, 16))
            return carry
        lax.fori_loop(1, 16, step, 0)

    def z_others(body):
        def step(k, carry):
            body(lax.rem(zi + k, 8))
            return carry
        lax.fori_loop(1, 8, step, 0)

    def sum_0(gr):
        core_copy(gr).start()

    def sum_1(gr):
        core_copy(gr).wait()

        def add(j):
            own = gs[gr][pl.ds(pl.multiple_of((core * 16 + j) * PIECES[gr], 16), PIECES[gr]), :]
            there = r0s[gr][piece_at(gr, j), :]
            hhs[gr][piece_at(gr, j), :] = (own.astype(F32) + there.astype(F32)).astype(BF16)

        def add_and_send(j):
            add(j)
            xy_copy(gr, j, me_xy).start()

        xy_others(add_and_send)
        add(me_xy)

    def sum_2(gr):
        def step(k, total):
            j = lax.rem(me_xy + k, 16)
            xy_copy(gr, me_xy, j).wait_recv()
            return total + rrs[gr][j].astype(F32)

        own = hhs[gr][piece_at(gr, me_xy), :].astype(F32)
        zs[gr][zi] = lax.fori_loop(1, 16, step, own).astype(BF16)
        z_others(lambda j: z_copy(gr, j, zi).start())

    def sum_3(gr):
        z_others(lambda j: z_copy(gr, zi, j).wait_recv())
        total = zs[gr][0].astype(F32)
        for j in range(1, 8):
            total = total + zs[gr][j].astype(F32)
        f[f_at(gr, core, me_xy), :] = total.astype(BF16)
        xy_others(lambda j: ag_copy(gr, j, me_xy).start())
        fw_copy(gr, me_xy, core).start()

    def sum_4(gr):
        def forward(j):
            ag_copy(gr, me_xy, j).wait_recv()
            fw_copy(gr, j, core).start()
        xy_others(forward)

    def sum_5(gr):
        def arrived(j, carry):
            fw_copy(gr, j, 1 - core).wait_recv()
            fw_copy(gr, j, core).wait_send()
            return carry
        lax.fori_loop(0, 16, arrived, 0)

    def sum_sent(gr):
        def sent(j):
            xy_copy(gr, j, me_xy).wait_send()
            ag_copy(gr, j, me_xy).wait_send()
        xy_others(sent)
        z_others(lambda j: z_copy(gr, j, zi).wait_send())

    def out_copy(gr):
        at = pl.ds(BASES[gr], 32 * PIECES[gr])
        return pltpu.make_async_copy(f.at[at], f_o.at[at], out_sem.at[gr])

    def aside(w):
        if w == 1:
            sum_1(2)

    def field_copy(i):
        return pltpu.make_async_copy((res_v, gt_v)[i], (res_o, gt_o)[i], out_sem.at[GROUPS + i])

    for gr in range(GROUPS):
        used = (12, 6)[gr % 2] * D
        gs[gr][used:, :] = jnp.zeros((32 * PIECES[gr] - used, 128), BF16)
    loads[0].wait()
    tile_to_windows(tok, cur)
    loads[2].wait()
    loads[6].wait()
    stage("prepare", lambda: prepare(0))
    loads[1].wait()
    tile_to_windows(ct, cw)
    pl.semaphore_wait(barrier, 29)
    halo_start(0, cw, 1)
    for i in (3, 4, 5):
        loads[i].wait()
    block_forward(0, cur, nxt, 1, 4)
    halo_start(1, nxt, 1)
    block_forward(0, cur, nxt, 0, 1)
    for i in (7, 8, 9, 10, 11):
        loads[i].wait()
    stage("prepare", lambda: prepare(1))
    unpack_shift(nxt, halo_f, cur, 1, (3,))
    block_forward(1, cur, out2, 3, 4)
    halo_finish(1, nxt, cur, 1, (0, 1, 2))
    block_forward(1, cur, out2, 0, 3)
    halo_start(2, out2, -1)
    halo_finish(0, cw, cur, 1)
    mlp_backward(1, cur, 0, 4)
    stage("mlp_terms", lambda: mlp_terms(1, 0, 0))
    sum_0(0)
    attention_backward(1, 0, 3)
    input_backward(1, cw, 0, 3)
    halo_start(3, cw, -1)
    sum_1(0)
    attention_backward(1, 3, 4)
    input_backward(1, cw, 3, 4)
    stage("attention_terms", lambda: attention_terms(1, 1, 0))
    sum_0(1)
    unpack_shift(cw, halo_f, nxt, -1, (0,))
    mlp_backward(0, nxt, 0, 1)
    sum_1(1)
    halo_finish(3, cw, nxt, -1, (1, 2, 3))
    mlp_backward(0, nxt, 1, 4)
    stage("mlp_terms", lambda: mlp_terms(0, 2, 0))
    sum_0(2)
    sum_2(0)
    attention_backward(0, 0, 4, aside)
    stage("attention_terms", lambda: attention_terms(0, 3, 0))
    sum_0(3)
    input_backward(0, cur, 0, 4)
    sum_1(3)
    windows_to_tile(cur, gt_v)
    field_copy(1).start()
    sum_2(1)
    halo_finish(2, out2, nxt, -1)
    windows_to_tile(nxt, res_v)
    field_copy(0).start()
    sum_3(0)
    sum_2(2)
    sum_3(1)
    sum_2(3)
    sum_4(0)
    sum_3(2)
    sum_4(1)
    sum_3(3)
    sum_5(0)
    out_copy(0).start()
    sum_4(2)
    sum_5(1)
    out_copy(1).start()
    sum_4(3)
    sum_5(2)
    out_copy(2).start()
    sum_5(3)
    out_copy(3).start()
    for gr in range(GROUPS):
        sum_sent(gr)
        out_copy(gr).wait()
    field_copy(0).wait()
    field_copy(1).wait()


def unpack_kernel(factor, f_in, res, gt, res_o, gt_o, *refs):
    outs, f, held, sems = refs[:8], refs[8], refs[9:17], refs[17]
    res_v, gt_v = refs[18], refs[19]
    copies = []
    fields = [
        pltpu.make_async_copy(res, res_v, sems.at[0]),
        pltpu.make_async_copy(gt, gt_v, sems.at[1]),
    ]
    parts = []
    for gr in range(GROUPS):
        at = pl.ds(BASES[gr], 32 * PIECES[gr])
        parts.append(pltpu.make_async_copy(f_in.at[at], f.at[at], sems.at[2 + gr]))
    for copy in parts + fields:
        copy.start()

    def tile(gr, i):
        at = BASES[gr] + i * D
        return f[at : at + D, :].astype(F32) * factor

    def attention_out(gr, i, qkv, proj):
        for n in range(3):
            two = jnp.concatenate([tile(gr, i + 2 * n), tile(gr, i + 2 * n + 1)], axis=1)
            qkv[:, D * n : D * n + D] = two[:, 0:D]
            proj[:, 64 * n : 64 * n + 64] = two[:, D:]

    def mlp_out(gr, i, up, down):
        for n in range(6):
            up[:, 128 * n : 128 * n + 128] = tile(gr, i + n)
            down[:, 128 * n : 128 * n + 128] = tile(gr, i + 6 + n)

    def send(first, count):
        for i in range(first, first + count):
            copy = pltpu.make_async_copy(held[i], outs[i], sems.at[2 + GROUPS + i])
            copy.start()
            copies.append(copy)

    parts[0].wait()
    mlp_out(0, 0, held[6], held[7])
    send(6, 2)
    for i, (held_f, out_f) in enumerate(((res_v, res_o), (gt_v, gt_o))):
        fields[i].wait()
        copy = pltpu.make_async_copy(held_f, out_f, sems.at[i])
        copy.start()
        copies.append(copy)
    parts[1].wait()
    attention_out(1, 0, held[4], held[5])
    send(4, 2)
    parts[2].wait()
    mlp_out(2, 0, held[2], held[3])
    send(2, 2)
    parts[3].wait()
    attention_out(3, 0, held[0], held[1])
    send(0, 2)
    for copy in copies:
        copy.wait()


def body(
    tokens, ga1, qkv1, proj1, gm1, up1, dn1, bias1,
    ga2, qkv2, proj2, gm2, up2, dn2, bias2, cotangent,
):
    vmem = pl.BlockSpec(memory_space=pltpu.VMEM)
    tile = jax.ShapeDtypeStruct((24, 24, D), BF16)

    def dma(*shape):
        return pltpu.SemaphoreType.DMA(shape)

    big = (
        tokens.reshape(24, 24, D), cotangent.reshape(24, 24, D),
        qkv1, proj1, up1, dn1.T, bias1.reshape(2, HEADS * WIN, WIN),
        qkv2, proj2, up2, dn2.T, bias2.reshape(2, HEADS * WIN, WIN),
    )
    anywhere = pl.BlockSpec(memory_space=pl.ANY)
    scratch = [
        pltpu.VMEM((2, D, 768), BF16),
        pltpu.VMEM((2, WIN, STACK), F32),
        pltpu.VMEM((2, 576, 1), F32),
        pltpu.VMEM((2, 576, D), F32),
        pltpu.VMEM((2, 576, D), F32),
        pltpu.VMEM((2, 576, D), BF16),
        pltpu.VMEM((2, 576, 768), BF16),
        pltpu.VMEM((2, 4, STACK, D), BF16),
        pltpu.VMEM((2, 4, WIN, STACK), BF16),
        pltpu.VMEM((2, 576, D), BF16),
        pltpu.VMEM((2, 576, D), F32),
        pltpu.VMEM((2, 576, D), F32),
        pltpu.VMEM((2, 576, D), BF16),
        pltpu.VMEM((2, 576, 768), BF16),
        pltpu.VMEM((2, 576, 768), BF16),
        pltpu.VMEM((24, 24, D), BF16),
        pltpu.VMEM((24, 24, D), BF16),
        pltpu.VMEM((ROWS, 128), BF16),
        pltpu.VMEM((576, D), F32),
        pltpu.VMEM((576, D), F32),
        pltpu.VMEM((576, D), F32),
        pltpu.VMEM((576, D), F32),
        pltpu.VMEM((HALO_ROWS, D), F32),
        pltpu.VMEM((HALO_ROWS, D), F32),
        pltpu.VMEM((4, HALO_ROWS, D), BF16),
        pltpu.VMEM((4, HALO_ROWS, D), BF16),
        pltpu.VMEM((576, D), BF16),
        pltpu.VMEM((576, 768), BF16),
        pltpu.VMEM((576, D), F32),
        pltpu.VMEM((576, D), BF16),
        pltpu.VMEM((576, D), BF16),
        pltpu.VMEM((4, STACK, D), BF16),
        pltpu.VMEM((4, WIN, STACK), BF16),
        pltpu.VMEM((576, 768), BF16),
        pltpu.VMEM((D, 768), F32),
        *[pltpu.VMEM((32 * r, 128), BF16) for r in PIECES],
        *[pltpu.VMEM((16 * r, 128), BF16) for r in PIECES],
        *[pltpu.VMEM((16 * r, 128), BF16) for r in PIECES],
        *[pltpu.VMEM((16, r, 128), BF16) for r in PIECES],
        *[pltpu.VMEM((8, r, 128), BF16) for r in PIECES],
        *[pltpu.VMEM(a.shape, BF16) for a in big],
        dma(4, 3), dma(4, 3),
        dma(GROUPS), dma(GROUPS),
        dma(GROUPS, 16), dma(GROUPS, 16),
        dma(GROUPS, 8), dma(GROUPS, 8),
        dma(GROUPS, 16), dma(GROUPS, 16),
        dma(GROUPS, 16), dma(GROUPS, 16),
        dma(GROUPS + 2), dma(12),
    ]
    res, gt, f = pl.pallas_call(
        megakernel,
        out_shape=(tile, tile, jax.ShapeDtypeStruct((ROWS, 128), BF16)),
        in_specs=[vmem] * 4 + [anywhere] * 12,
        out_specs=(anywhere,) * 3,
        scratch_shapes=scratch,
        compiler_params=pltpu.CompilerParams(
            collective_id=0, has_side_effects=True, vmem_limit_bytes=60 * 1024 * 1024
        ),
    )(
        ga1, gm1, ga2, gm2, *big
    )
    one = [
        jax.ShapeDtypeStruct((D, 3 * D), F32),
        jax.ShapeDtypeStruct((D, D), F32),
        jax.ShapeDtypeStruct((D, 4 * D), F32),
        jax.ShapeDtypeStruct((D, 4 * D), F32),
    ]
    outs = list(pl.pallas_call(
        functools.partial(unpack_kernel, 1.0 / math.sqrt(256.0 * 576.0)),
        out_shape=[tile, tile] + one + one,
        in_specs=[anywhere] * 3,
        out_specs=[anywhere] * 10,
        scratch_shapes=[pltpu.VMEM((ROWS, 128), BF16)]
        + [pltpu.VMEM(s.shape, F32) for s in one + one]
        + [dma(10 + GROUPS), pltpu.VMEM(tile.shape, BF16), pltpu.VMEM(tile.shape, BF16)],
        compiler_params=pltpu.CompilerParams(vmem_limit_bytes=60 * 1024 * 1024),
    )(f, res, gt))
    shape = (2, 12, 24, D)
    terms = outs[2:5] + [outs[5].T] + outs[6:9] + [outs[9].T]
    return (outs[0].reshape(shape), outs[1].reshape(shape)) + tuple(terms)


def solution(mesh):
    grid = P(None, "lat", "lon", None)
    bias = P("lat", None, None, None, None)
    block = (P(), P(), P(), P(), P(), P(), bias)
    return jax.shard_map(
        body,
        mesh=mesh,
        in_specs=(grid,) + block + block + (grid,),
        out_specs=(grid, grid) + (P(),) * 8,
        check_vma=False,
    )
```

```python
import functools
import math

import jax
import jax.numpy as jnp
from jax import lax
from jax.experimental import pallas as pl
from jax.experimental.pallas import tpu as pltpu
from jax.sharding import PartitionSpec as P

F32 = jnp.float32
BF16 = jnp.bfloat16
HEADS = 6
WIN = 144
PAD = 11
D = 192
STACK = 896
SCALE = 32 ** -0.5
CHUNKS = ((0, 256), (256, 512), (512, 768), (768, 896))
PIECES = (80, 32, 80, 32)
BASES = (0, 32 * 80, 32 * 112, 32 * 192)
ROWS = 32 * 224
GROUPS = 4
MESH = pl.DeviceIdType.MESH


def dot_nn(a, b):
    return lax.dot_general(a, b, (((1,), (0,)), ((), ())), preferred_element_type=F32)


def dot_nt(a, b):
    return lax.dot_general(a, b, (((1,), (1,)), ((), ())), preferred_element_type=F32)


def dot_tn(a, b):
    return lax.dot_general(a, b, (((0,), (0,)), ((), ())), preferred_element_type=F32)


def stage(name, work):
    work()


def win_rows(w):
    return pl.ds(pl.multiple_of(w * WIN, 16), WIN)


def lane_mean(x):
    return dot_nn(x, jnp.ones((D, D), BF16)) * (1.0 / D)


def normalise(x, exact):
    high = x.astype(BF16)
    mean = lane_mean(high)
    if not exact:
        mean = mean + lane_mean((x - high.astype(F32)).astype(BF16))
    centred = x - mean
    r = lax.rsqrt(lane_mean((centred * centred).astype(BF16)) + 1e-05)
    return centred * r, r


def normalise_back(dy, xhat, r):
    m1 = lane_mean(dy.astype(BF16))
    m2 = lane_mean((dy * xhat).astype(BF16))
    return r * (dy - m1 - xhat * m2)


def live_column(first_row, limit):
    n = lax.broadcasted_iota(jnp.int32, (WIN, 1), 0)
    m = jnp.where(n >= 72, n - 72, n)
    row = jnp.zeros_like(m)
    for i in range(1, 6):
        row = row + jnp.where(m >= 12 * i, 1, 0)
    pos = row + first_row
    return jnp.where((pos >= 0) & (pos < limit), 1.0, 0.0).astype(F32)


def head_mask(h, dtype):
    lane = lax.broadcasted_iota(jnp.int32, (1, D), 1)
    inside = (lane >= 32 * h) & (lane < 32 * h + 32)
    return jnp.where(inside, 1.0, 0.0).astype(F32).astype(dtype)


def own_lanes(o):
    lane = lax.broadcasted_iota(jnp.int32, (1, 128), 1)
    left = o[3 * WIN : 4 * WIN, 0:128]
    for h in (2, 1, 0):
        left = jnp.where(lane < 32 * h + 32, o[WIN * h : WIN * h + WIN, 0:128], left)
    right = jnp.where(
        lane[:, 0:64] < 32, o[4 * WIN : 5 * WIN, 128:D], o[5 * WIN : 6 * WIN, 128:D]
    )
    return jnp.concatenate([left, right], axis=1)


def tile_to_windows(src, dst):
    for level in range(2):
        for row in range(12):
            x = src[level * 12 + row].astype(F32)
            for wc in range(2):
                at = ((row // 6) * 2 + wc) * WIN + level * 72 + (row % 6) * 12
                dst[at : at + 12, :] = x[12 * wc : 12 * wc + 12, :]


def windows_to_tile(src, dst):
    for level in range(2):
        for row in range(12):
            parts = []
            for wc in range(2):
                at = ((row // 6) * 2 + wc) * WIN + level * 72 + (row % 6) * 12
                parts.append(src[at : at + 12, :])
            dst[level * 12 + row] = jnp.concatenate(parts, axis=0).astype(BF16)


def place(level, row, col):
    return ((row // 6) * 2 + col // 12) * WIN + level * 72 + (row % 6) * 12 + col % 12


def pack_halo(src, pack, out, row0, row1, col0, col1):
    at = 0
    for rows, cols in ((row0, col1), (row1, col0), (row1, col1)):
        for level in range(2):
            for row in rows:
                for col in cols:
                    p = place(level, row, col)
                    pack[at : at + 6, :] = src[p : p + 6, :]
                    at += 6
        at = (at + 15) // 16 * 16
    out[...] = pack[...].astype(BF16)


HALO_ROWS = 112 + 112 + 48
HALO_PARTS = ((0, 112), (112, 112), (224, 48))


def unpack_shift(src, halo, dst, step, windows):
    for level in range(2):
        for row in range(12):
            for col in range(0, 24, 6):
                if (row // 6) * 2 + col // 12 not in windows:
                    continue
                r, c = row - 3 * step, col - 6 * step
                r_in, c_in = 0 <= r < 12, 0 <= c < 24
                if r_in and c_in:
                    p = place(level, r, c)
                    piece = src[p : p + 6, :]
                else:
                    if r_in:
                        i = r if step > 0 else r - 3
                        at = (level * 9 + i) * 6
                    elif c_in:
                        i = row if step > 0 else row - 9
                        j = c if step > 0 else c - 6
                        at = 112 + (level * 3 + i) * 18 + j
                    else:
                        i = row if step > 0 else row - 9
                        at = 224 + (level * 3 + i) * 6
                    piece = halo[at : at + 6, :]
                q = place(level, row, col)
                dst[q : q + 6, :] = piece


def megakernel(
    ga1, gm1, ga2, gm2, tok, ct, qkv1, proj1, up1, dn1, bias1, qkv2, proj2, up2, dn2, bias2,
    res_o, gt_o, f_o,
    wp, bt, alive, xhat1, r1, normed, proj_all, qm, pt, att, xhat2, r2, second, hidden, gp,
    res_v, gt_v, f, cur, nxt, out2, cw, pack, halo_f, halo_out, halo_in,
    dtot, du, dres, dres_b, datt, dom, dst_, dqkv, w5, *refs
):
    gs, r0s, hhs, rrs, zs = (refs[GROUPS * i : GROUPS * i + GROUPS] for i in range(5))
    held, sems = refs[5 * GROUPS : 5 * GROUPS + 12], refs[5 * GROUPS + 12 :]
    (
        halo_send, halo_recv, core_send, core_recv, xy_send, xy_recv, z_send, z_recv,
        ag_send, ag_recv, fw_send, fw_recv, out_sem, in_sem,
    ) = sems
    loads = [
        pltpu.make_async_copy(there, here, in_sem.at[i])
        for i, (there, here) in enumerate(
            zip((tok, ct, qkv1, proj1, up1, dn1, bias1, qkv2, proj2, up2, dn2, bias2), held)
        )
    ]
    for i in (0, 2, 6, 1, 3, 4, 5, 7, 11, 8, 9, 10):
        loads[i].start()
    tok, ct, qkv1, proj1, up1, dn1, bias1, qkv2, proj2, up2, dn2, bias2 = held
    lon = lax.axis_index("lon")
    lat = lax.axis_index("lat")
    core = lax.rem(lon, 2)
    chip = lon // 2
    y_hi = lat // 8
    zi = lax.rem(lat, 8)
    me_xy = y_hi * 8 + chip

    def sibling():
        return {"lon": chip * 2 + 1 - core, "lat": lat}

    def xy_dev(j):
        return {"lon": lax.rem(j, 8) * 2 + core, "lat": (j // 8) * 8 + zi}

    def z_dev(j):
        return {"lon": lon, "lat": y_hi * 8 + j}

    def near(step_lon, step_lat):
        return {
            "lon": lax.rem(lon + step_lon + 16, 16),
            "lat": lax.rem(lat + step_lat + 16, 16),
        }

    barrier = pltpu.get_barrier_semaphore()

    def greet(device):
        pl.semaphore_signal(barrier, inc=1, device_id=device, device_id_type=MESH)

    greet(sibling())
    for k in range(1, 16):
        greet(xy_dev(lax.rem(me_xy + k, 16)))
    for k in range(1, 8):
        greet(z_dev(lax.rem(zi + k, 8)))
    for s in (1, -1):
        greet(near(s, 0))
        greet(near(0, s))
        greet(near(s, s))

    def halo_copy(x, part, step):
        first, count = HALO_PARTS[part]
        device = near(step if part != 1 else 0, step if part != 0 else 0)
        return pltpu.make_async_remote_copy(
            src_ref=halo_out.at[x, pl.ds(first, count)],
            dst_ref=halo_in.at[x, pl.ds(first, count)],
            send_sem=halo_send.at[x, part],
            recv_sem=halo_recv.at[x, part],
            device_id=device,
            device_id_type=MESH,
        )

    def halo_start(x, src, step):
        if step > 0:
            pack_halo(src, pack, halo_out.at[x], range(0, 9), range(9, 12), (0, 6, 12), (18,))
        else:
            pack_halo(src, pack, halo_out.at[x], range(3, 12), range(0, 3), (6, 12, 18), (0,))
        for part in range(3):
            halo_copy(x, part, step).start()

    def halo_finish(x, src, dst, step, windows=(0, 1, 2, 3)):
        for part in range(3):
            halo_copy(x, part, step).wait()
        outside = jnp.where(lat == (0 if step > 0 else 15), 0.0, 1.0).astype(F32)
        halo_f[0:112, :] = halo_in[x, 0:112].astype(F32)
        halo_f[112:, :] = halo_in[x, 112:].astype(F32) * outside
        unpack_shift(src, halo_f, dst, step, windows)

    limit = 16 * 12 - PAD
    starts = (lat * 12, lat * 12 - 3)
    weights = (
        (ga1, qkv1, proj1, gm1, up1, dn1, bias1),
        (ga2, qkv2, proj2, gm2, up2, dn2, bias2),
    )

    def prepare(b):
        ga, wqkv, wproj, gm, wup, wdn, bias = weights[b]
        wp[b] = jnp.zeros((D, 768), BF16)
        for i in range(3):
            part = wqkv[...].astype(F32)[:, D * i : D * i + D]
            wp[b, :, 256 * i : 256 * i + D] = part.astype(BF16)
        rows_i = lax.broadcasted_iota(jnp.int32, (WIN, WIN), 0)
        cols_i = lax.broadcasted_iota(jnp.int32, (WIN, WIN), 1)
        eye = jnp.where(rows_i == cols_i, 1.0, 0.0).astype(F32).astype(BF16)
        for wr in range(2):
            here = live_column(starts[b] + 6 * wr, limit)
            penalty = (here - 1.0) * 30000.0
            for wc in range(2):
                alive[b, (2 * wr + wc) * WIN : (2 * wr + wc + 1) * WIN, :] = here
            bt[wr, :, 0:864] = dot_nt(eye, bias[wr]) + penalty
            bt[wr, :, 864:] = jnp.zeros((WIN, STACK - 864), F32)

    def block_forward(b, x_in, x_out, lo, hi):
        ga, wqkv, wproj, gm, wup, wdn, bias = weights[b]
        gain_a = ga[...].reshape(1, D)
        gain_m = gm[...].reshape(1, D)

        span = slice(lo * WIN, hi * WIN)

        def f_qkv():
            xh, r = normalise(x_in[span, :], True)
            xhat1[b, span, :] = xh
            r1[b, span, :] = r
            normed[b, span, :] = (xh * gain_a).astype(BF16)
            proj_all[b, span, :] = dot_nn(normed[b, span, :], wp[b]).astype(BF16)

        stage("f_qkv", f_qkv)

        def f_att(w):
            rows = win_rows(w)
            wr = w // 2
            q = proj_all[b, rows, 0:D]
            k = proj_all[b, rows, 256 : 256 + D]
            v = proj_all[b, rows, 512 : 512 + D]
            for h in range(HEADS):
                qm[b, w, WIN * h : WIN * h + WIN, :] = q * head_mask(h, BF16)
            qm[b, w, 864:, :] = jnp.zeros((STACK - 864, D), BF16)
            for c0, c1 in CHUNKS:
                s = dot_nt(k, qm[b, w, c0:c1, :]) * SCALE + bt[wr, :, c0:c1]
                e = jnp.exp(s - jnp.max(s, axis=0, keepdims=True))
                total = jnp.sum(e, axis=0, keepdims=True)
                pt[b, w, :, c0:c1] = (e * (1.0 / total)).astype(BF16)
            o = dot_tn(pt[b, w], v)
            a = own_lanes(o)
            att[b, rows, :] = a.astype(BF16)

        stage("f_att", lambda: [f_att(w) for w in range(lo, hi)])

        def f_mlp():
            resid = x_in[span, :] + dot_nn(att[b, span, :], wproj[...])
            x_out[span, :] = resid
            xh, r = normalise(resid, False)
            xhat2[b, span, :] = xh
            r2[b, span, :] = r
            second[b, span, :] = (xh * gain_m).astype(BF16)
            c = math.sqrt(2.0 / math.pi)
            for n in range(3):
                at = slice(256 * n, 256 * n + 256)
                u = dot_nn(second[b, span, :], wup[:, at])
                u2 = u * u
                t = jnp.tanh(u * (c + (c * 0.044715) * u2))
                half = 0.5 + 0.5 * t
                hidden[b, span, at] = (u * half).astype(BF16)
                slope = half + u * (half * (1.0 - half)) * (2 * c + (6 * c * 0.044715) * u2)
                gp[b, span, at] = slope.astype(BF16)
            out = (x_out[span, :] + dot_nt(hidden[b, span, :], wdn[...])) * alive[b, span, :]
            x_out[span, :] = out.astype(BF16).astype(F32)

        stage("f_mlp", f_mlp)

    def mlp_backward(b, d_out, lo, hi):
        ga, wqkv, wproj, gm, wup, wdn, bias = weights[b]
        gain_m = gm[...].reshape(1, D)

        span = slice(lo * WIN, hi * WIN)

        def b_mlp():
            dtb = (d_out[span, :] * alive[b, span, :]).astype(BF16)
            dtot[span, :] = dtb
            for n in range(3):
                at = slice(256 * n, 256 * n + 256)
                dh = dot_nn(dtot[span, :], wdn[:, at]).astype(BF16).astype(F32)
                du[span, at] = (dh * gp[b, span, at].astype(F32)).astype(BF16)
            dy = dot_nt(du[span, :], wup[...]).astype(BF16).astype(F32) * gain_m
            dr = dtot[span, :].astype(F32) + normalise_back(dy, xhat2[b, span, :], r2[b, span, :])
            dres[span, :] = dr
            dres_b[span, :] = dr.astype(BF16)
            datt[span, :] = dot_nt(dres_b[span, :], wproj[...]).astype(BF16)

        stage("b_mlp", b_mlp)

    def attention_backward(b, lo, hi, between=None):
        def b_att(w):
            rows = win_rows(w)
            k = proj_all[b, rows, 256 : 256 + D]
            v = proj_all[b, rows, 512 : 512 + D]
            do = datt[rows, :]
            for h in range(HEADS):
                dom[w, WIN * h : WIN * h + WIN, :] = do * head_mask(h, BF16)
            dom[w, 864:, :] = jnp.zeros((STACK - 864, D), BF16)
            for c0, c1 in CHUNKS:
                dp = dot_nt(v, dom[w, c0:c1, :]).astype(BF16).astype(F32)
                p = pt[b, w, :, c0:c1].astype(F32)
                delta = jnp.sum(p * dp, axis=0, keepdims=True)
                dst_[w, :, c0:c1] = (p * (dp - delta)).astype(BF16)
            zeros = jnp.zeros((WIN, 64), BF16)
            dqkv[rows, 512 : 512 + D] = dot_nn(pt[b, w], dom[w]).astype(BF16)
            dqkv[rows, 256 : 256 + D] = (dot_nn(dst_[w], qm[b, w]) * SCALE).astype(BF16)
            o = dot_tn(dst_[w], k)
            a = own_lanes(o)
            dqkv[rows, 0:D] = (a * SCALE).astype(BF16)
            for i in range(3):
                dqkv[rows, 256 * i + D : 256 * i + 256] = zeros

            if between is not None:
                between(w)

        stage("b_att", lambda: [b_att(w) for w in range(lo, hi)])

    def input_backward(b, d_in, lo, hi):
        gain_a = weights[b][0][...].reshape(1, D)

        span = slice(lo * WIN, hi * WIN)

        def b_qkv():
            dy = dot_nt(dqkv[span, :], wp[b]).astype(BF16).astype(F32) * gain_a
            dx = dres[span, :] + normalise_back(dy, xhat1[b, span, :], r1[b, span, :])
            d_in[span, :] = dx.astype(BF16).astype(F32)

        stage("b_qkv", b_qkv)

    def put(gr, at, matrix):
        for i in range(matrix.shape[1] // 128):
            rows = slice((at + i) * D, (at + i + 1) * D)
            gs[gr][rows, :] = matrix[:, 128 * i : 128 * i + 128].astype(BF16)

    def mlp_terms(b, gr):
        put(gr, 0, dot_tn(second[b], du[...]))
        put(gr, 6, dot_tn(dtot[...], hidden[b]))
        pr = dot_tn(att[b], dres_b[...])
        put(gr, 12, pr[:, 0:128])
        w5[b, :, 576:640] = pr[:, 128:D]

    def attention_terms(b, gr):
        terms = dot_tn(normed[b], dqkv[...])
        for i in range(3):
            w5[b, :, D * i : D * i + D] = terms[:, 256 * i : 256 * i + D]
        put(gr, 0, w5[b])

    def remote(src, dst, send, recv, device):
        return pltpu.make_async_remote_copy(
            src_ref=src, dst_ref=dst, send_sem=send, recv_sem=recv,
            device_id=device, device_id_type=MESH,
        )

    def piece_at(gr, j):
        return pl.ds(pl.multiple_of(j * PIECES[gr], 16), PIECES[gr])

    def f_at(gr, c, j):
        return pl.ds(pl.multiple_of(BASES[gr] + (c * 16 + j) * PIECES[gr], 16), PIECES[gr])

    def core_copy(gr):
        rows = 16 * PIECES[gr]
        there = pl.ds(pl.multiple_of((1 - core) * rows, 16), rows)
        return remote(gs[gr].at[there], r0s[gr], core_send.at[gr], core_recv.at[gr], sibling())

    def half_at(gr, c):
        rows = 16 * PIECES[gr]
        return pl.ds(pl.multiple_of(BASES[gr] + c * rows, 16), rows)

    def xy_copy(gr, k):
        j = lax.rem(me_xy + k, 16)
        return remote(
            hhs[gr].at[piece_at(gr, j)], rrs[gr].at[k - 1],
            xy_send.at[gr], xy_recv.at[gr], xy_dev(j),
        )

    def xy_all(gr):
        every = rrs[gr].at[pl.ds(0, 15)]
        return remote(every, every, xy_send.at[gr], xy_recv.at[gr], xy_dev(lax.rem(me_xy + 1, 16)))

    def z_copy(gr, k):
        here = zs[gr].at[zi]
        return remote(here, here, z_send.at[gr], z_recv.at[gr], z_dev(lax.rem(zi + k, 8)))

    def z_all(gr):
        every = zs[gr].at[pl.ds(0, 7)]
        return remote(every, every, z_send.at[gr], z_recv.at[gr], z_dev(lax.rem(zi + 1, 8)))

    def ag_copy(gr, k):
        here = f.at[f_at(gr, core, me_xy)]
        return remote(here, here, ag_send.at[gr], ag_recv.at[gr], xy_dev(lax.rem(me_xy + k, 16)))

    def ag_all(gr):
        every = f.at[pl.ds(BASES[gr], 15 * PIECES[gr])]
        return remote(every, every, ag_send.at[gr], ag_recv.at[gr], xy_dev(lax.rem(me_xy + 1, 16)))

    def fw_copy(gr, c):
        half = f.at[half_at(gr, c)]
        return remote(half, half, fw_send.at[gr], fw_recv.at[gr], sibling())

    def each(count, body):
        def step(k, carry):
            body(k)
            return carry
        lax.fori_loop(1, count, step, 0)

    def sum_0(gr):
        core_copy(gr).start()

    def sum_1(gr):
        core_copy(gr).wait()

        def add(j):
            own = gs[gr][pl.ds(pl.multiple_of((core * 16 + j) * PIECES[gr], 16), PIECES[gr]), :]
            there = r0s[gr][piece_at(gr, j), :]
            hhs[gr][piece_at(gr, j), :] = (own.astype(F32) + there.astype(F32)).astype(BF16)

        def add_and_send(k):
            add(lax.rem(me_xy + k, 16))
            xy_copy(gr, k).start()

        each(16, add_and_send)
        add(me_xy)

    def sum_2(gr):
        total = hhs[gr][piece_at(gr, me_xy), :].astype(F32)
        xy_all(gr).wait_recv()
        for k in range(15):
            total = total + rrs[gr][k].astype(F32)
        zs[gr][zi] = total.astype(BF16)
        each(8, lambda k: z_copy(gr, k).start())

    def sum_3(gr):
        z_all(gr).wait_recv()
        total = zs[gr][0].astype(F32)
        for j in range(1, 8):
            total = total + zs[gr][j].astype(F32)
        f[f_at(gr, core, me_xy), :] = total.astype(BF16)
        each(16, lambda k: ag_copy(gr, k).start())

    def sum_4(gr):
        ag_all(gr).wait_recv()
        fw_copy(gr, core).start()

    def sum_5(gr):
        fw_copy(gr, 1 - core).wait_recv()

    def sum_sent(gr):
        xy_all(gr).wait_send()
        z_all(gr).wait_send()
        ag_all(gr).wait_send()
        fw_copy(gr, core).wait_send()

    def out_copy(gr):
        at = pl.ds(BASES[gr], 32 * PIECES[gr])
        return pltpu.make_async_copy(f.at[at], f_o.at[at], out_sem.at[gr])

    def aside(w):
        if w == 1:
            sum_1(2)

    def field_copy(i):
        return pltpu.make_async_copy((res_v, gt_v)[i], (res_o, gt_o)[i], out_sem.at[GROUPS + i])

    for gr in range(GROUPS):
        used = (13, 5)[gr % 2] * D
        gs[gr][used:, :] = jnp.zeros((32 * PIECES[gr] - used, 128), BF16)
    loads[0].wait()
    tile_to_windows(tok, cur)
    loads[2].wait()
    loads[6].wait()
    stage("prepare", lambda: prepare(0))
    loads[1].wait()
    tile_to_windows(ct, cw)
    pl.semaphore_wait(barrier, 29)
    halo_start(0, cw, 1)
    for i in (3, 4, 5):
        loads[i].wait()
    block_forward(0, cur, nxt, 1, 4)
    halo_start(1, nxt, 1)
    block_forward(0, cur, nxt, 0, 1)
    for i in (7, 8, 9, 10, 11):
        loads[i].wait()
    stage("prepare", lambda: prepare(1))
    unpack_shift(nxt, halo_f, cur, 1, (3,))
    block_forward(1, cur, out2, 3, 4)
    halo_finish(1, nxt, cur, 1, (0, 1, 2))
    block_forward(1, cur, out2, 0, 3)
    halo_start(2, out2, -1)
    halo_finish(0, cw, cur, 1)
    mlp_backward(1, cur, 0, 4)
    stage("mlp_terms", lambda: mlp_terms(1, 0))
    sum_0(0)
    attention_backward(1, 0, 3)
    input_backward(1, cw, 0, 3)
    halo_start(3, cw, -1)
    sum_1(0)
    attention_backward(1, 3, 4)
    input_backward(1, cw, 3, 4)
    stage("attention_terms", lambda: attention_terms(1, 1))
    sum_0(1)
    unpack_shift(cw, halo_f, nxt, -1, (0,))
    mlp_backward(0, nxt, 0, 1)
    sum_1(1)
    halo_finish(3, cw, nxt, -1, (1, 2, 3))
    mlp_backward(0, nxt, 1, 4)
    stage("mlp_terms", lambda: mlp_terms(0, 2))
    sum_0(2)
    sum_2(0)
    attention_backward(0, 0, 4, aside)
    stage("attention_terms", lambda: attention_terms(0, 3))
    sum_0(3)
    input_backward(0, cur, 0, 4)
    sum_1(3)
    windows_to_tile(cur, gt_v)
    field_copy(1).start()
    sum_2(1)
    halo_finish(2, out2, nxt, -1)
    windows_to_tile(nxt, res_v)
    field_copy(0).start()
    sum_3(0)
    sum_2(2)
    sum_3(1)
    sum_2(3)
    sum_4(0)
    sum_3(2)
    sum_4(1)
    sum_3(3)
    sum_5(0)
    out_copy(0).start()
    sum_4(2)
    sum_5(1)
    out_copy(1).start()
    sum_4(3)
    sum_5(2)
    out_copy(2).start()
    sum_5(3)
    out_copy(3).start()
    for gr in range(GROUPS):
        sum_sent(gr)
        out_copy(gr).wait()
    field_copy(0).wait()
    field_copy(1).wait()


def unpack_kernel(factor, f_in, res, gt, res_o, gt_o, *refs):
    outs, f, held, sems = refs[:8], refs[8], refs[9:17], refs[17]
    res_v, gt_v = refs[18], refs[19]
    copies = []
    fields = [
        pltpu.make_async_copy(res, res_v, sems.at[0]),
        pltpu.make_async_copy(gt, gt_v, sems.at[1]),
    ]
    parts = []
    for gr in range(GROUPS):
        at = pl.ds(BASES[gr], 32 * PIECES[gr])
        parts.append(pltpu.make_async_copy(f_in.at[at], f.at[at], sems.at[2 + gr]))
    for copy in parts + fields:
        copy.start()

    def tile(gr, i):
        at = BASES[gr] + i * D
        return f[at : at + D, :].astype(F32) * factor

    def mlp_out(gr, up, down, proj):
        for n in range(6):
            up[:, 128 * n : 128 * n + 128] = tile(gr, n)
            down[:, 128 * n : 128 * n + 128] = tile(gr, n + 6)
        proj[:, 0:128] = tile(gr, 12)

    def attention_out(gr, qkv, proj):
        for n in range(4):
            qkv[:, 128 * n : 128 * n + 128] = tile(gr, n)
        last = tile(gr, 4)
        qkv[:, 512:576] = last[:, 0:64]
        proj[:, 128:D] = last[:, 64:128]

    def send(first, count):
        for i in range(first, first + count):
            copy = pltpu.make_async_copy(held[i], outs[i], sems.at[2 + GROUPS + i])
            copy.start()
            copies.append(copy)

    parts[0].wait()
    mlp_out(0, held[6], held[7], held[5])
    send(6, 2)
    for i, (held_f, out_f) in enumerate(((res_v, res_o), (gt_v, gt_o))):
        fields[i].wait()
        copy = pltpu.make_async_copy(held_f, out_f, sems.at[i])
        copy.start()
        copies.append(copy)
    parts[1].wait()
    attention_out(1, held[4], held[5])
    send(4, 2)
    parts[2].wait()
    mlp_out(2, held[2], held[3], held[1])
    send(2, 2)
    parts[3].wait()
    attention_out(3, held[0], held[1])
    send(0, 2)
    for copy in copies:
        copy.wait()


def body(
    tokens, ga1, qkv1, proj1, gm1, up1, dn1, bias1,
    ga2, qkv2, proj2, gm2, up2, dn2, bias2, cotangent,
):
    vmem = pl.BlockSpec(memory_space=pltpu.VMEM)
    tile = jax.ShapeDtypeStruct((24, 24, D), BF16)

    def dma(*shape):
        return pltpu.SemaphoreType.DMA(shape)

    big = (
        tokens.reshape(24, 24, D), cotangent.reshape(24, 24, D),
        qkv1, proj1, up1, dn1.T, bias1.reshape(2, HEADS * WIN, WIN),
        qkv2, proj2, up2, dn2.T, bias2.reshape(2, HEADS * WIN, WIN),
    )
    anywhere = pl.BlockSpec(memory_space=pl.ANY)
    scratch = [
        pltpu.VMEM((2, D, 768), BF16),
        pltpu.VMEM((2, WIN, STACK), F32),
        pltpu.VMEM((2, 576, 1), F32),
        pltpu.VMEM((2, 576, D), F32),
        pltpu.VMEM((2, 576, D), F32),
        pltpu.VMEM((2, 576, D), BF16),
        pltpu.VMEM((2, 576, 768), BF16),
        pltpu.VMEM((2, 4, STACK, D), BF16),
        pltpu.VMEM((2, 4, WIN, STACK), BF16),
        pltpu.VMEM((2, 576, D), BF16),
        pltpu.VMEM((2, 576, D), F32),
        pltpu.VMEM((2, 576, D), F32),
        pltpu.VMEM((2, 576, D), BF16),
        pltpu.VMEM((2, 576, 768), BF16),
        pltpu.VMEM((2, 576, 768), BF16),
        pltpu.VMEM((24, 24, D), BF16),
        pltpu.VMEM((24, 24, D), BF16),
        pltpu.VMEM((ROWS, 128), BF16),
        pltpu.VMEM((576, D), F32),
        pltpu.VMEM((576, D), F32),
        pltpu.VMEM((576, D), F32),
        pltpu.VMEM((576, D), F32),
        pltpu.VMEM((HALO_ROWS, D), F32),
        pltpu.VMEM((HALO_ROWS, D), F32),
        pltpu.VMEM((4, HALO_ROWS, D), BF16),
        pltpu.VMEM((4, HALO_ROWS, D), BF16),
        pltpu.VMEM((576, D), BF16),
        pltpu.VMEM((576, 768), BF16),
        pltpu.VMEM((576, D), F32),
        pltpu.VMEM((576, D), BF16),
        pltpu.VMEM((576, D), BF16),
        pltpu.VMEM((4, STACK, D), BF16),
        pltpu.VMEM((4, WIN, STACK), BF16),
        pltpu.VMEM((576, 768), BF16),
        pltpu.VMEM((2, D, 640), F32),
        *[pltpu.VMEM((32 * r, 128), BF16) for r in PIECES],
        *[pltpu.VMEM((16 * r, 128), BF16) for r in PIECES],
        *[pltpu.VMEM((16 * r, 128), BF16) for r in PIECES],
        *[pltpu.VMEM((16, r, 128), BF16) for r in PIECES],
        *[pltpu.VMEM((8, r, 128), BF16) for r in PIECES],
        *[pltpu.VMEM(a.shape, BF16) for a in big],
        dma(4, 3), dma(4, 3),
        dma(GROUPS), dma(GROUPS),
        dma(GROUPS), dma(GROUPS),
        dma(GROUPS), dma(GROUPS),
        dma(GROUPS), dma(GROUPS),
        dma(GROUPS), dma(GROUPS),
        dma(GROUPS + 2), dma(12),
    ]
    res, gt, f = pl.pallas_call(
        megakernel,
        out_shape=(tile, tile, jax.ShapeDtypeStruct((ROWS, 128), BF16)),
        in_specs=[vmem] * 4 + [anywhere] * 12,
        out_specs=(anywhere,) * 3,
        scratch_shapes=scratch,
        compiler_params=pltpu.CompilerParams(
            collective_id=0, has_side_effects=True, vmem_limit_bytes=60 * 1024 * 1024
        ),
    )(
        ga1, gm1, ga2, gm2, *big
    )
    one = [
        jax.ShapeDtypeStruct((D, 3 * D), F32),
        jax.ShapeDtypeStruct((D, D), F32),
        jax.ShapeDtypeStruct((D, 4 * D), F32),
        jax.ShapeDtypeStruct((D, 4 * D), F32),
    ]
    outs = list(pl.pallas_call(
        functools.partial(unpack_kernel, 1.0 / math.sqrt(256.0 * 576.0)),
        out_shape=[tile, tile] + one + one,
        in_specs=[anywhere] * 3,
        out_specs=[anywhere] * 10,
        scratch_shapes=[pltpu.VMEM((ROWS, 128), BF16)]
        + [pltpu.VMEM(s.shape, F32) for s in one + one]
        + [dma(10 + GROUPS), pltpu.VMEM(tile.shape, BF16), pltpu.VMEM(tile.shape, BF16)],
        compiler_params=pltpu.CompilerParams(vmem_limit_bytes=60 * 1024 * 1024),
    )(f, res, gt))
    shape = (2, 12, 24, D)
    terms = outs[2:5] + [outs[5].T] + outs[6:9] + [outs[9].T]
    return (outs[0].reshape(shape), outs[1].reshape(shape)) + tuple(terms)


def solution(mesh):
    grid = P(None, "lat", "lon", None)
    bias = P("lat", None, None, None, None)
    block = (P(), P(), P(), P(), P(), P(), bias)
    return jax.shard_map(
        body,
        mesh=mesh,
        in_specs=(grid,) + block + block + (grid,),
        out_specs=(grid, grid) + (P(),) * 8,
        check_vma=False,
    )
```

```python
import functools
import math

import jax
import jax.numpy as jnp
from jax import lax
from jax.experimental import pallas as pl
from jax.experimental.pallas import tpu as pltpu
from jax.sharding import PartitionSpec as P

F32 = jnp.float32
BF16 = jnp.bfloat16
HEADS = 6
WIN = 144
PAD = 11
D = 192
STACK = 896
SCALE = 32 ** -0.5
CHUNKS = ((0, 256), (256, 512), (512, 768), (768, 896))
PIECES = (80, 32, 80, 32)
BASES = (0, 32 * 80, 32 * 112, 32 * 192)
ROWS = 32 * 224
GROUPS = 4
MESH = pl.DeviceIdType.MESH


def dot_nn(a, b):
    return lax.dot_general(a, b, (((1,), (0,)), ((), ())), preferred_element_type=F32)


def dot_nt(a, b):
    return lax.dot_general(a, b, (((1,), (1,)), ((), ())), preferred_element_type=F32)


def dot_tn(a, b):
    return lax.dot_general(a, b, (((0,), (0,)), ((), ())), preferred_element_type=F32)


def stage(name, work):
    work()


def win_rows(w):
    return pl.ds(pl.multiple_of(w * WIN, 16), WIN)


def lane_mean(x):
    return dot_nn(x, jnp.ones((D, D), BF16)) * (1.0 / D)


def normalise(x, exact):
    high = x.astype(BF16)
    mean = lane_mean(high)
    if not exact:
        mean = mean + lane_mean((x - high.astype(F32)).astype(BF16))
    centred = x - mean
    r = lax.rsqrt(lane_mean((centred * centred).astype(BF16)) + 1e-05)
    return centred * r, r


def normalise_back(dy, xhat, r):
    m1 = lane_mean(dy.astype(BF16))
    m2 = lane_mean((dy * xhat).astype(BF16))
    return r * (dy - m1 - xhat * m2)


def live_column(first_row, limit):
    n = lax.broadcasted_iota(jnp.int32, (WIN, 1), 0)
    m = jnp.where(n >= 72, n - 72, n)
    row = jnp.zeros_like(m)
    for i in range(1, 6):
        row = row + jnp.where(m >= 12 * i, 1, 0)
    pos = row + first_row
    return jnp.where((pos >= 0) & (pos < limit), 1.0, 0.0).astype(F32)


def head_mask(h, dtype):
    lane = lax.broadcasted_iota(jnp.int32, (1, D), 1)
    inside = (lane >= 32 * h) & (lane < 32 * h + 32)
    return jnp.where(inside, 1.0, 0.0).astype(F32).astype(dtype)


def own_lanes(o):
    lane = lax.broadcasted_iota(jnp.int32, (1, 128), 1)
    left = o[3 * WIN : 4 * WIN, 0:128]
    for h in (2, 1, 0):
        left = jnp.where(lane < 32 * h + 32, o[WIN * h : WIN * h + WIN, 0:128], left)
    right = jnp.where(
        lane[:, 0:64] < 32, o[4 * WIN : 5 * WIN, 128:D], o[5 * WIN : 6 * WIN, 128:D]
    )
    return jnp.concatenate([left, right], axis=1)


def tile_to_windows(src, dst):
    for level in range(2):
        for row in range(12):
            x = src[level * 12 + row].astype(F32)
            for wc in range(2):
                at = ((row // 6) * 2 + wc) * WIN + level * 72 + (row % 6) * 12
                dst[at : at + 12, :] = x[12 * wc : 12 * wc + 12, :]


def windows_to_tile(src, dst):
    for level in range(2):
        for row in range(12):
            parts = []
            for wc in range(2):
                at = ((row // 6) * 2 + wc) * WIN + level * 72 + (row % 6) * 12
                parts.append(src[at : at + 12, :])
            dst[level * 12 + row] = jnp.concatenate(parts, axis=0).astype(BF16)


def place(level, row, col):
    return ((row // 6) * 2 + col // 12) * WIN + level * 72 + (row % 6) * 12 + col % 12


def pack_halo(src, pack, out, row0, row1, col0, col1, parts):
    for part in parts:
        rows, cols = ((row0, col1), (row1, col0), (row1, col1))[part]
        first, count = HALO_PARTS[part]
        at = first
        for level in range(2):
            for row in rows:
                for col in cols:
                    p = place(level, row, col)
                    pack[at : at + 6, :] = src[p : p + 6, :]
                    at += 6
        out[first : first + count, :] = pack[first : first + count, :].astype(BF16)


HALO_ROWS = 112 + 112 + 48
HALO_PARTS = ((0, 112), (112, 112), (224, 48))


def unpack_shift(src, halo, dst, step, windows):
    for level in range(2):
        for row in range(12):
            for col in range(0, 24, 6):
                if (row // 6) * 2 + col // 12 not in windows:
                    continue
                r, c = row - 3 * step, col - 6 * step
                r_in, c_in = 0 <= r < 12, 0 <= c < 24
                if r_in and c_in:
                    p = place(level, r, c)
                    piece = src[p : p + 6, :]
                else:
                    if r_in:
                        i = r if step > 0 else r - 3
                        at = (level * 9 + i) * 6
                    elif c_in:
                        i = row if step > 0 else row - 9
                        j = c if step > 0 else c - 6
                        at = 112 + (level * 3 + i) * 18 + j
                    else:
                        i = row if step > 0 else row - 9
                        at = 224 + (level * 3 + i) * 6
                    piece = halo[at : at + 6, :]
                q = place(level, row, col)
                dst[q : q + 6, :] = piece


def megakernel(
    ga1, gm1, ga2, gm2, tok, ct, qkv1, proj1, up1, dn1, bias1, qkv2, proj2, up2, dn2, bias2,
    res_o, gt_o, f_o,
    wp, bt, alive, xhat1, r1, normed, proj_all, qm, pt, att, xhat2, r2, second, hidden, gp,
    res_v, gt_v, f, cur, nxt, out2, cw, pack, halo_f, halo_out, halo_in,
    dtot, du, dres, dres_b, datt, dom, dst_, dqkv, w5, *refs
):
    gs, r0s, hhs, rrs, zs = (refs[GROUPS * i : GROUPS * i + GROUPS] for i in range(5))
    held, sems = refs[5 * GROUPS : 5 * GROUPS + 12], refs[5 * GROUPS + 12 :]
    (
        halo_send, halo_recv, core_send, core_recv, xy_send, xy_recv, z_send, z_recv,
        ag_send, ag_recv, fw_send, fw_recv, out_sem, in_sem,
    ) = sems
    loads = [
        pltpu.make_async_copy(there, here, in_sem.at[i])
        for i, (there, here) in enumerate(
            zip((tok, ct, qkv1, proj1, up1, dn1, bias1, qkv2, proj2, up2, dn2, bias2), held)
        )
    ]
    for i in (0, 2, 6, 1, 3, 4, 5, 7, 11, 8, 9, 10):
        loads[i].start()
    tok, ct, qkv1, proj1, up1, dn1, bias1, qkv2, proj2, up2, dn2, bias2 = held
    lon = lax.axis_index("lon")
    lat = lax.axis_index("lat")
    core = lax.rem(lon, 2)
    chip = lon // 2
    y_hi = lat // 8
    zi = lax.rem(lat, 8)
    me_xy = y_hi * 8 + chip

    def sibling():
        return {"lon": chip * 2 + 1 - core, "lat": lat}

    def xy_dev(j):
        return {"lon": lax.rem(j, 8) * 2 + core, "lat": (j // 8) * 8 + zi}

    def z_dev(j):
        return {"lon": lon, "lat": y_hi * 8 + j}

    def near(step_lon, step_lat):
        return {
            "lon": lax.rem(lon + step_lon + 16, 16),
            "lat": lax.rem(lat + step_lat + 16, 16),
        }

    barrier = pltpu.get_barrier_semaphore()

    def greet(device):
        pl.semaphore_signal(barrier, inc=1, device_id=device, device_id_type=MESH)

    greet(sibling())
    for k in range(1, 16):
        greet(xy_dev(lax.rem(me_xy + k, 16)))
    for k in range(1, 8):
        greet(z_dev(lax.rem(zi + k, 8)))
    for s in (1, -1):
        greet(near(s, 0))
        greet(near(0, s))
        greet(near(s, s))

    def halo_copy(x, part, step):
        first, count = HALO_PARTS[part]
        device = near(step if part != 1 else 0, step if part != 0 else 0)
        return pltpu.make_async_remote_copy(
            src_ref=halo_out.at[x, pl.ds(first, count)],
            dst_ref=halo_in.at[x, pl.ds(first, count)],
            send_sem=halo_send.at[x, part],
            recv_sem=halo_recv.at[x, part],
            device_id=device,
            device_id_type=MESH,
        )

    def halo_start(x, src, step, parts=(0, 1, 2)):
        if step > 0:
            where = (range(0, 9), range(9, 12), (0, 6, 12), (18,))
        else:
            where = (range(3, 12), range(0, 3), (6, 12, 18), (0,))
        pack_halo(src, pack, halo_out.at[x], *where, parts)
        for part in parts:
            halo_copy(x, part, step).start()

    def halo_finish(x, src, dst, step, windows=(0, 1, 2, 3)):
        for part in range(3):
            halo_copy(x, part, step).wait()
        outside = jnp.where(lat == (0 if step > 0 else 15), 0.0, 1.0).astype(F32)
        halo_f[0:112, :] = halo_in[x, 0:112].astype(F32)
        halo_f[112:, :] = halo_in[x, 112:].astype(F32) * outside
        unpack_shift(src, halo_f, dst, step, windows)

    limit = 16 * 12 - PAD
    starts = (lat * 12, lat * 12 - 3)
    weights = (
        (ga1, qkv1, proj1, gm1, up1, dn1, bias1),
        (ga2, qkv2, proj2, gm2, up2, dn2, bias2),
    )

    def prepare(b):
        ga, wqkv, wproj, gm, wup, wdn, bias = weights[b]
        wp[b] = jnp.zeros((D, 768), BF16)
        for i in range(3):
            part = wqkv[...].astype(F32)[:, D * i : D * i + D]
            wp[b, :, 256 * i : 256 * i + D] = part.astype(BF16)
        rows_i = lax.broadcasted_iota(jnp.int32, (WIN, WIN), 0)
        cols_i = lax.broadcasted_iota(jnp.int32, (WIN, WIN), 1)
        eye = jnp.where(rows_i == cols_i, 1.0, 0.0).astype(F32).astype(BF16)
        for wr in range(2):
            here = live_column(starts[b] + 6 * wr, limit)
            penalty = (here - 1.0) * 30000.0
            for wc in range(2):
                alive[b, (2 * wr + wc) * WIN : (2 * wr + wc + 1) * WIN, :] = here
            bt[wr, :, 0:864] = dot_nt(eye, bias[wr]) + penalty
            bt[wr, :, 864:] = jnp.zeros((WIN, STACK - 864), F32)

    def block_forward(b, x_in, x_out, lo, hi):
        ga, wqkv, wproj, gm, wup, wdn, bias = weights[b]
        gain_a = ga[...].reshape(1, D)
        gain_m = gm[...].reshape(1, D)

        span = slice(lo * WIN, hi * WIN)

        def f_qkv():
            xh, r = normalise(x_in[span, :], True)
            xhat1[b, span, :] = xh
            r1[b, span, :] = r
            normed[b, span, :] = (xh * gain_a).astype(BF16)
            proj_all[b, span, :] = dot_nn(normed[b, span, :], wp[b]).astype(BF16)

        stage("f_qkv", f_qkv)

        def f_att(w):
            rows = win_rows(w)
            wr = w // 2
            q = proj_all[b, rows, 0:D]
            k = proj_all[b, rows, 256 : 256 + D]
            v = proj_all[b, rows, 512 : 512 + D]
            for h in range(HEADS):
                qm[b, w, WIN * h : WIN * h + WIN, :] = q * head_mask(h, BF16)
            qm[b, w, 864:, :] = jnp.zeros((STACK - 864, D), BF16)
            for c0, c1 in CHUNKS:
                s = dot_nt(k, qm[b, w, c0:c1, :]) * SCALE + bt[wr, :, c0:c1]
                e = jnp.exp(s - jnp.max(s, axis=0, keepdims=True))
                total = jnp.sum(e, axis=0, keepdims=True)
                pt[b, w, :, c0:c1] = (e * (1.0 / total)).astype(BF16)
            o = dot_tn(pt[b, w], v)
            a = own_lanes(o)
            att[b, rows, :] = a.astype(BF16)

        stage("f_att", lambda: [f_att(w) for w in range(lo, hi)])

        def f_mlp():
            resid = x_in[span, :] + dot_nn(att[b, span, :], wproj[...])
            x_out[span, :] = resid
            xh, r = normalise(resid, False)
            xhat2[b, span, :] = xh
            r2[b, span, :] = r
            second[b, span, :] = (xh * gain_m).astype(BF16)
            c = math.sqrt(2.0 / math.pi)
            for n in range(3):
                at = slice(256 * n, 256 * n + 256)
                u = dot_nn(second[b, span, :], wup[:, at])
                u2 = u * u
                t = jnp.tanh(u * (c + (c * 0.044715) * u2))
                half = 0.5 + 0.5 * t
                hidden[b, span, at] = (u * half).astype(BF16)
                slope = half + u * (half * (1.0 - half)) * (2 * c + (6 * c * 0.044715) * u2)
                gp[b, span, at] = slope.astype(BF16)
            out = (x_out[span, :] + dot_nt(hidden[b, span, :], wdn[...])) * alive[b, span, :]
            x_out[span, :] = out.astype(BF16).astype(F32)

        stage("f_mlp", f_mlp)

    def mlp_backward(b, d_out, lo, hi):
        ga, wqkv, wproj, gm, wup, wdn, bias = weights[b]
        gain_m = gm[...].reshape(1, D)

        span = slice(lo * WIN, hi * WIN)

        def b_mlp():
            dtb = (d_out[span, :] * alive[b, span, :]).astype(BF16)
            dtot[span, :] = dtb
            for n in range(3):
                at = slice(256 * n, 256 * n + 256)
                dh = dot_nn(dtot[span, :], wdn[:, at]).astype(BF16).astype(F32)
                du[span, at] = (dh * gp[b, span, at].astype(F32)).astype(BF16)
            dy = dot_nt(du[span, :], wup[...]).astype(BF16).astype(F32) * gain_m
            dr = dtot[span, :].astype(F32) + normalise_back(dy, xhat2[b, span, :], r2[b, span, :])
            dres[span, :] = dr
            dres_b[span, :] = dr.astype(BF16)
            datt[span, :] = dot_nt(dres_b[span, :], wproj[...]).astype(BF16)

        stage("b_mlp", b_mlp)

    def attention_backward(b, lo, hi, between=None):
        def b_att(w):
            rows = win_rows(w)
            k = proj_all[b, rows, 256 : 256 + D]
            v = proj_all[b, rows, 512 : 512 + D]
            do = datt[rows, :]
            for h in range(HEADS):
                dom[w, WIN * h : WIN * h + WIN, :] = do * head_mask(h, BF16)
            dom[w, 864:, :] = jnp.zeros((STACK - 864, D), BF16)
            for c0, c1 in CHUNKS:
                dp = dot_nt(v, dom[w, c0:c1, :]).astype(BF16).astype(F32)
                p = pt[b, w, :, c0:c1].astype(F32)
                delta = jnp.sum(p * dp, axis=0, keepdims=True)
                dst_[w, :, c0:c1] = (p * (dp - delta)).astype(BF16)
            zeros = jnp.zeros((WIN, 64), BF16)
            dqkv[rows, 512 : 512 + D] = dot_nn(pt[b, w], dom[w]).astype(BF16)
            dqkv[rows, 256 : 256 + D] = (dot_nn(dst_[w], qm[b, w]) * SCALE).astype(BF16)
            o = dot_tn(dst_[w], k)
            a = own_lanes(o)
            dqkv[rows, 0:D] = (a * SCALE).astype(BF16)
            for i in range(3):
                dqkv[rows, 256 * i + D : 256 * i + 256] = zeros

            if between is not None:
                between(w)

        stage("b_att", lambda: [b_att(w) for w in range(lo, hi)])

    def input_backward(b, d_in, lo, hi):
        gain_a = weights[b][0][...].reshape(1, D)

        span = slice(lo * WIN, hi * WIN)

        def b_qkv():
            dy = dot_nt(dqkv[span, :], wp[b]).astype(BF16).astype(F32) * gain_a
            dx = dres[span, :] + normalise_back(dy, xhat1[b, span, :], r1[b, span, :])
            d_in[span, :] = dx.astype(BF16).astype(F32)

        stage("b_qkv", b_qkv)

    def put(gr, at, matrix):
        for i in range(matrix.shape[1] // 128):
            rows = slice((at + i) * D, (at + i + 1) * D)
            gs[gr][rows, :] = matrix[:, 128 * i : 128 * i + 128].astype(BF16)

    def mlp_terms(b, gr):
        put(gr, 0, dot_tn(second[b], du[...]))
        put(gr, 6, dot_tn(dtot[...], hidden[b]))
        pr = dot_tn(att[b], dres_b[...])
        put(gr, 12, pr[:, 0:128])
        w5[b, :, 576:640] = pr[:, 128:D]

    def attention_terms(b, gr):
        terms = dot_tn(normed[b], dqkv[...])
        for i in range(3):
            w5[b, :, D * i : D * i + D] = terms[:, 256 * i : 256 * i + D]
        put(gr, 0, w5[b])

    def remote(src, dst, send, recv, device):
        return pltpu.make_async_remote_copy(
            src_ref=src, dst_ref=dst, send_sem=send, recv_sem=recv,
            device_id=device, device_id_type=MESH,
        )

    def piece_at(gr, j):
        return pl.ds(pl.multiple_of(j * PIECES[gr], 16), PIECES[gr])

    def f_at(gr, c, j):
        return pl.ds(pl.multiple_of(BASES[gr] + (c * 16 + j) * PIECES[gr], 16), PIECES[gr])

    def core_copy(gr):
        rows = 16 * PIECES[gr]
        there = pl.ds(pl.multiple_of((1 - core) * rows, 16), rows)
        return remote(gs[gr].at[there], r0s[gr], core_send.at[gr], core_recv.at[gr], sibling())

    def half_at(gr, c):
        rows = 16 * PIECES[gr]
        return pl.ds(pl.multiple_of(BASES[gr] + c * rows, 16), rows)

    def xy_copy(gr, k):
        j = lax.rem(me_xy + k, 16)
        return remote(
            hhs[gr].at[piece_at(gr, j)], rrs[gr].at[k - 1],
            xy_send.at[gr], xy_recv.at[gr], xy_dev(j),
        )

    def xy_all(gr):
        every = rrs[gr].at[pl.ds(0, 15)]
        return remote(every, every, xy_send.at[gr], xy_recv.at[gr], xy_dev(lax.rem(me_xy + 1, 16)))

    def z_copy(gr, k):
        here = zs[gr].at[zi]
        return remote(here, here, z_send.at[gr], z_recv.at[gr], z_dev(lax.rem(zi + k, 8)))

    def z_all(gr):
        every = zs[gr].at[pl.ds(0, 7)]
        return remote(every, every, z_send.at[gr], z_recv.at[gr], z_dev(lax.rem(zi + 1, 8)))

    def ag_copy(gr, k):
        here = f.at[f_at(gr, core, me_xy)]
        return remote(here, here, ag_send.at[gr], ag_recv.at[gr], xy_dev(lax.rem(me_xy + k, 16)))

    def ag_all(gr):
        every = f.at[pl.ds(BASES[gr], 15 * PIECES[gr])]
        return remote(every, every, ag_send.at[gr], ag_recv.at[gr], xy_dev(lax.rem(me_xy + 1, 16)))

    def fw_copy(gr, c):
        half = f.at[half_at(gr, c)]
        return remote(half, half, fw_send.at[gr], fw_recv.at[gr], sibling())

    def each(count, body):
        def step(k, carry):
            body(k)
            return carry
        lax.fori_loop(1, count, step, 0)

    def sum_0(gr):
        core_copy(gr).start()

    def sum_1(gr):
        core_copy(gr).wait()

        def add(j):
            own = gs[gr][pl.ds(pl.multiple_of((core * 16 + j) * PIECES[gr], 16), PIECES[gr]), :]
            there = r0s[gr][piece_at(gr, j), :]
            hhs[gr][piece_at(gr, j), :] = (own.astype(F32) + there.astype(F32)).astype(BF16)

        def add_and_send(k):
            add(lax.rem(me_xy + k, 16))
            xy_copy(gr, k).start()

        each(16, add_and_send)
        add(me_xy)

    def sum_2(gr):
        total = hhs[gr][piece_at(gr, me_xy), :].astype(F32)
        xy_all(gr).wait_recv()
        for k in range(15):
            total = total + rrs[gr][k].astype(F32)
        zs[gr][zi] = total.astype(BF16)
        each(8, lambda k: z_copy(gr, k).start())

    def sum_3(gr):
        z_all(gr).wait_recv()
        total = zs[gr][0].astype(F32)
        for j in range(1, 8):
            total = total + zs[gr][j].astype(F32)
        f[f_at(gr, core, me_xy), :] = total.astype(BF16)
        each(16, lambda k: ag_copy(gr, k).start())

    def sum_4(gr):
        ag_all(gr).wait_recv()
        fw_copy(gr, core).start()

    def sum_5(gr):
        fw_copy(gr, 1 - core).wait_recv()

    def sum_sent(gr):
        xy_all(gr).wait_send()
        z_all(gr).wait_send()
        ag_all(gr).wait_send()
        fw_copy(gr, core).wait_send()

    def out_copy(gr):
        at = pl.ds(BASES[gr], 32 * PIECES[gr])
        return pltpu.make_async_copy(f.at[at], f_o.at[at], out_sem.at[gr])

    def aside(w):
        if w == 1:
            sum_1(2)
        if w == 2:
            sum_2(0)

    def field_copy(i):
        return pltpu.make_async_copy((res_v, gt_v)[i], (res_o, gt_o)[i], out_sem.at[GROUPS + i])

    for gr in range(GROUPS):
        used = (13, 5)[gr % 2] * D
        gs[gr][used:, :] = jnp.zeros((32 * PIECES[gr] - used, 128), BF16)
    loads[0].wait()
    tile_to_windows(tok, cur)
    loads[2].wait()
    loads[6].wait()
    stage("prepare", lambda: prepare(0))
    for i in (3, 4, 5):
        loads[i].wait()
    block_forward(0, cur, nxt, 2, 4)
    pl.semaphore_wait(barrier, 29)
    halo_start(1, nxt, 1, (1, 2))
    block_forward(0, cur, nxt, 0, 2)
    halo_start(1, nxt, 1, (0,))
    loads[1].wait()
    tile_to_windows(ct, cw)
    halo_start(0, cw, 1)
    for i in (7, 8, 9, 10, 11):
        loads[i].wait()
    stage("prepare", lambda: prepare(1))
    unpack_shift(nxt, halo_f, cur, 1, (3,))
    block_forward(1, cur, out2, 3, 4)
    halo_finish(1, nxt, cur, 1, (0, 1, 2))
    block_forward(1, cur, out2, 0, 3)
    halo_start(2, out2, -1)
    halo_finish(0, cw, cur, 1)
    mlp_backward(1, cur, 0, 4)
    stage("mlp_terms", lambda: mlp_terms(1, 0))
    sum_0(0)
    attention_backward(1, 0, 2)
    input_backward(1, cw, 0, 2)
    halo_start(3, cw, -1, (1, 2))
    attention_backward(1, 2, 3)
    input_backward(1, cw, 2, 3)
    halo_start(3, cw, -1, (0,))
    sum_1(0)
    attention_backward(1, 3, 4)
    input_backward(1, cw, 3, 4)
    stage("attention_terms", lambda: attention_terms(1, 1))
    sum_0(1)
    unpack_shift(cw, halo_f, nxt, -1, (0,))
    mlp_backward(0, nxt, 0, 1)
    sum_1(1)
    halo_finish(3, cw, nxt, -1, (1, 2, 3))
    mlp_backward(0, nxt, 1, 4)
    stage("mlp_terms", lambda: mlp_terms(0, 2))
    sum_0(2)
    attention_backward(0, 0, 4, aside)
    stage("attention_terms", lambda: attention_terms(0, 3))
    sum_0(3)
    input_backward(0, cur, 0, 4)
    sum_1(3)
    windows_to_tile(cur, gt_v)
    field_copy(1).start()
    sum_2(1)
    halo_finish(2, out2, nxt, -1)
    windows_to_tile(nxt, res_v)
    field_copy(0).start()
    sum_3(0)
    sum_2(2)
    sum_2(3)
    sum_3(1)
    sum_4(0)
    sum_3(2)
    sum_4(1)
    sum_3(3)
    sum_5(0)
    out_copy(0).start()
    sum_4(2)
    sum_5(1)
    out_copy(1).start()
    sum_4(3)
    sum_5(2)
    out_copy(2).start()
    sum_5(3)
    out_copy(3).start()
    for gr in range(GROUPS):
        sum_sent(gr)
        out_copy(gr).wait()
    field_copy(0).wait()
    field_copy(1).wait()


def unpack_kernel(factor, f_in, res, gt, res_o, gt_o, *refs):
    outs, f, held, sems = refs[:8], refs[8], refs[9:17], refs[17]
    res_v, gt_v = refs[18], refs[19]
    copies = []
    fields = [
        pltpu.make_async_copy(res, res_v, sems.at[0]),
        pltpu.make_async_copy(gt, gt_v, sems.at[1]),
    ]
    parts = []
    for gr in range(GROUPS):
        at = pl.ds(BASES[gr], 32 * PIECES[gr])
        parts.append(pltpu.make_async_copy(f_in.at[at], f.at[at], sems.at[2 + gr]))
    for copy in parts + fields:
        copy.start()

    def tile(gr, i):
        at = BASES[gr] + i * D
        return f[at : at + D, :].astype(F32) * factor

    def mlp_out(gr, up, down, proj):
        for n in range(6):
            up[:, 128 * n : 128 * n + 128] = tile(gr, n)
            down[:, 128 * n : 128 * n + 128] = tile(gr, n + 6)
        proj[:, 0:128] = tile(gr, 12)

    def attention_out(gr, qkv, proj):
        for n in range(4):
            qkv[:, 128 * n : 128 * n + 128] = tile(gr, n)
        last = tile(gr, 4)
        qkv[:, 512:576] = last[:, 0:64]
        proj[:, 128:D] = last[:, 64:128]

    def send(first, count):
        for i in range(first, first + count):
            copy = pltpu.make_async_copy(held[i], outs[i], sems.at[2 + GROUPS + i])
            copy.start()
            copies.append(copy)

    parts[0].wait()
    mlp_out(0, held[6], held[7], held[5])
    send(6, 2)
    for i, (held_f, out_f) in enumerate(((res_v, res_o), (gt_v, gt_o))):
        fields[i].wait()
        copy = pltpu.make_async_copy(held_f, out_f, sems.at[i])
        copy.start()
        copies.append(copy)
    parts[1].wait()
    attention_out(1, held[4], held[5])
    send(4, 2)
    parts[2].wait()
    mlp_out(2, held[2], held[3], held[1])
    send(2, 2)
    parts[3].wait()
    attention_out(3, held[0], held[1])
    send(0, 2)
    for copy in copies:
        copy.wait()


def body(
    tokens, ga1, qkv1, proj1, gm1, up1, dn1, bias1,
    ga2, qkv2, proj2, gm2, up2, dn2, bias2, cotangent,
):
    vmem = pl.BlockSpec(memory_space=pltpu.VMEM)
    tile = jax.ShapeDtypeStruct((24, 24, D), BF16)

    def dma(*shape):
        return pltpu.SemaphoreType.DMA(shape)

    big = (
        tokens.reshape(24, 24, D), cotangent.reshape(24, 24, D),
        qkv1, proj1, up1, dn1.T, bias1.reshape(2, HEADS * WIN, WIN),
        qkv2, proj2, up2, dn2.T, bias2.reshape(2, HEADS * WIN, WIN),
    )
    anywhere = pl.BlockSpec(memory_space=pl.ANY)
    scratch = [
        pltpu.VMEM((2, D, 768), BF16),
        pltpu.VMEM((2, WIN, STACK), F32),
        pltpu.VMEM((2, 576, 1), F32),
        pltpu.VMEM((2, 576, D), F32),
        pltpu.VMEM((2, 576, D), F32),
        pltpu.VMEM((2, 576, D), BF16),
        pltpu.VMEM((2, 576, 768), BF16),
        pltpu.VMEM((2, 4, STACK, D), BF16),
        pltpu.VMEM((2, 4, WIN, STACK), BF16),
        pltpu.VMEM((2, 576, D), BF16),
        pltpu.VMEM((2, 576, D), F32),
        pltpu.VMEM((2, 576, D), F32),
        pltpu.VMEM((2, 576, D), BF16),
        pltpu.VMEM((2, 576, 768), BF16),
        pltpu.VMEM((2, 576, 768), BF16),
        pltpu.VMEM((24, 24, D), BF16),
        pltpu.VMEM((24, 24, D), BF16),
        pltpu.VMEM((ROWS, 128), BF16),
        pltpu.VMEM((576, D), F32),
        pltpu.VMEM((576, D), F32),
        pltpu.VMEM((576, D), F32),
        pltpu.VMEM((576, D), F32),
        pltpu.VMEM((HALO_ROWS, D), F32),
        pltpu.VMEM((HALO_ROWS, D), F32),
        pltpu.VMEM((4, HALO_ROWS, D), BF16),
        pltpu.VMEM((4, HALO_ROWS, D), BF16),
        pltpu.VMEM((576, D), BF16),
        pltpu.VMEM((576, 768), BF16),
        pltpu.VMEM((576, D), F32),
        pltpu.VMEM((576, D), BF16),
        pltpu.VMEM((576, D), BF16),
        pltpu.VMEM((4, STACK, D), BF16),
        pltpu.VMEM((4, WIN, STACK), BF16),
        pltpu.VMEM((576, 768), BF16),
        pltpu.VMEM((2, D, 640), F32),
        *[pltpu.VMEM((32 * r, 128), BF16) for r in PIECES],
        *[pltpu.VMEM((16 * r, 128), BF16) for r in PIECES],
        *[pltpu.VMEM((16 * r, 128), BF16) for r in PIECES],
        *[pltpu.VMEM((16, r, 128), BF16) for r in PIECES],
        *[pltpu.VMEM((8, r, 128), BF16) for r in PIECES],
        *[pltpu.VMEM(a.shape, BF16) for a in big],
        dma(4, 3), dma(4, 3),
        dma(GROUPS), dma(GROUPS),
        dma(GROUPS), dma(GROUPS),
        dma(GROUPS), dma(GROUPS),
        dma(GROUPS), dma(GROUPS),
        dma(GROUPS), dma(GROUPS),
        dma(GROUPS + 2), dma(12),
    ]
    res, gt, f = pl.pallas_call(
        megakernel,
        out_shape=(tile, tile, jax.ShapeDtypeStruct((ROWS, 128), BF16)),
        in_specs=[vmem] * 4 + [anywhere] * 12,
        out_specs=(anywhere,) * 3,
        scratch_shapes=scratch,
        compiler_params=pltpu.CompilerParams(
            collective_id=0, has_side_effects=True, vmem_limit_bytes=60 * 1024 * 1024
        ),
    )(
        ga1, gm1, ga2, gm2, *big
    )
    one = [
        jax.ShapeDtypeStruct((D, 3 * D), F32),
        jax.ShapeDtypeStruct((D, D), F32),
        jax.ShapeDtypeStruct((D, 4 * D), F32),
        jax.ShapeDtypeStruct((D, 4 * D), F32),
    ]
    outs = list(pl.pallas_call(
        functools.partial(unpack_kernel, 1.0 / math.sqrt(256.0 * 576.0)),
        out_shape=[tile, tile] + one + one,
        in_specs=[anywhere] * 3,
        out_specs=[anywhere] * 10,
        scratch_shapes=[pltpu.VMEM((ROWS, 128), BF16)]
        + [pltpu.VMEM(s.shape, F32) for s in one + one]
        + [dma(10 + GROUPS), pltpu.VMEM(tile.shape, BF16), pltpu.VMEM(tile.shape, BF16)],
        compiler_params=pltpu.CompilerParams(vmem_limit_bytes=60 * 1024 * 1024),
    )(f, res, gt))
    shape = (2, 12, 24, D)
    terms = outs[2:5] + [outs[5].T] + outs[6:9] + [outs[9].T]
    return (outs[0].reshape(shape), outs[1].reshape(shape)) + tuple(terms)


def solution(mesh):
    grid = P(None, "lat", "lon", None)
    bias = P("lat", None, None, None, None)
    block = (P(), P(), P(), P(), P(), P(), bias)
    return jax.shard_map(
        body,
        mesh=mesh,
        in_specs=(grid,) + block + block + (grid,),
        out_specs=(grid, grid) + (P(),) * 8,
        check_vma=False,
    )
```

```python
import functools
import math

import jax
import jax.numpy as jnp
from jax import lax
from jax.experimental import pallas as pl
from jax.experimental.pallas import tpu as pltpu
from jax.sharding import PartitionSpec as P

F32 = jnp.float32
BF16 = jnp.bfloat16
HEADS = 6
WIN = 144
PAD = 11
D = 192
STACK = 896
SCALE = 32 ** -0.5
CHUNKS = ((0, 256), (256, 512), (512, 768), (768, 896))
PIECES = (80, 32, 80, 32)
BASES = (0, 32 * 80, 32 * 112, 32 * 192)
ROWS = 32 * 224
GROUPS = 4
MESH = pl.DeviceIdType.MESH


def dot_nn(a, b):
    return lax.dot_general(a, b, (((1,), (0,)), ((), ())), preferred_element_type=F32)


def dot_nt(a, b):
    return lax.dot_general(a, b, (((1,), (1,)), ((), ())), preferred_element_type=F32)


def dot_tn(a, b):
    return lax.dot_general(a, b, (((0,), (0,)), ((), ())), preferred_element_type=F32)


def stage(name, work):
    work()


def win_rows(w):
    return pl.ds(pl.multiple_of(w * WIN, 16), WIN)


def lane_mean(x):
    return dot_nn(x, jnp.ones((D, D), BF16)) * (1.0 / D)


def normalise(x, exact):
    high = x.astype(BF16)
    mean = lane_mean(high)
    if not exact:
        mean = mean + lane_mean((x - high.astype(F32)).astype(BF16))
    centred = x - mean
    r = lax.rsqrt(lane_mean((centred * centred).astype(BF16)) + 1e-05)
    return centred * r, r


def normalise_back(dy, xhat, r):
    m1 = lane_mean(dy.astype(BF16))
    m2 = lane_mean((dy * xhat).astype(BF16))
    return r * (dy - m1 - xhat * m2)


def live_column(first_row, limit):
    n = lax.broadcasted_iota(jnp.int32, (WIN, 1), 0)
    m = jnp.where(n >= 72, n - 72, n)
    row = jnp.zeros_like(m)
    for i in range(1, 6):
        row = row + jnp.where(m >= 12 * i, 1, 0)
    pos = row + first_row
    return jnp.where((pos >= 0) & (pos < limit), 1.0, 0.0).astype(F32)


def head_mask(h, dtype):
    lane = lax.broadcasted_iota(jnp.int32, (1, D), 1)
    inside = (lane >= 32 * h) & (lane < 32 * h + 32)
    return jnp.where(inside, 1.0, 0.0).astype(F32).astype(dtype)


def own_lanes(o):
    lane = lax.broadcasted_iota(jnp.int32, (1, 128), 1)
    left = o[3 * WIN : 4 * WIN, 0:128]
    for h in (2, 1, 0):
        left = jnp.where(lane < 32 * h + 32, o[WIN * h : WIN * h + WIN, 0:128], left)
    right = jnp.where(
        lane[:, 0:64] < 32, o[4 * WIN : 5 * WIN, 128:D], o[5 * WIN : 6 * WIN, 128:D]
    )
    return jnp.concatenate([left, right], axis=1)


def tile_to_windows(src, dst):
    for level in range(2):
        for row in range(12):
            x = src[level * 12 + row].astype(F32)
            for wc in range(2):
                at = ((row // 6) * 2 + wc) * WIN + level * 72 + (row % 6) * 12
                dst[at : at + 12, :] = x[12 * wc : 12 * wc + 12, :]


def windows_to_tile(src, dst):
    for level in range(2):
        for row in range(12):
            parts = []
            for wc in range(2):
                at = ((row // 6) * 2 + wc) * WIN + level * 72 + (row % 6) * 12
                parts.append(src[at : at + 12, :])
            dst[level * 12 + row] = jnp.concatenate(parts, axis=0).astype(BF16)


def place(level, row, col):
    return ((row // 6) * 2 + col // 12) * WIN + level * 72 + (row % 6) * 12 + col % 12


def pack_halo(src, pack, out, row0, row1, col0, col1, parts):
    for part in parts:
        rows, cols = ((row0, col1), (row1, col0), (row1, col1))[part]
        first, count = HALO_PARTS[part]
        at = first
        for level in range(2):
            for row in rows:
                for col in cols:
                    p = place(level, row, col)
                    pack[at : at + 6, :] = src[p : p + 6, :]
                    at += 6
        out[first : first + count, :] = pack[first : first + count, :].astype(BF16)


HALO_ROWS = 112 + 112 + 48
HALO_PARTS = ((0, 112), (112, 112), (224, 48))


def unpack_shift(src, halo, dst, step, windows):
    for level in range(2):
        for row in range(12):
            for col in range(0, 24, 6):
                if (row // 6) * 2 + col // 12 not in windows:
                    continue
                r, c = row - 3 * step, col - 6 * step
                r_in, c_in = 0 <= r < 12, 0 <= c < 24
                if r_in and c_in:
                    p = place(level, r, c)
                    piece = src[p : p + 6, :]
                else:
                    if r_in:
                        i = r if step > 0 else r - 3
                        at = (level * 9 + i) * 6
                    elif c_in:
                        i = row if step > 0 else row - 9
                        j = c if step > 0 else c - 6
                        at = 112 + (level * 3 + i) * 18 + j
                    else:
                        i = row if step > 0 else row - 9
                        at = 224 + (level * 3 + i) * 6
                    piece = halo[at : at + 6, :]
                q = place(level, row, col)
                dst[q : q + 6, :] = piece


def megakernel(
    ga1, gm1, ga2, gm2, tok, ct, qkv1, proj1, up1, dn1, bias1, qkv2, proj2, up2, dn2, bias2,
    res_o, gt_o, f_o,
    wp, bt, alive, xhat1, r1, normed, proj_all, qm, pt, att, xhat2, r2, second, hidden, gp,
    res_v, gt_v, f, cur, nxt, out2, cw, pack, halo_f, halo_out, halo_in,
    dtot, du, dres, dres_b, datt, dom, dst_, dqkv, w5, *refs
):
    gs, r0s, hhs, rrs, zs = (refs[GROUPS * i : GROUPS * i + GROUPS] for i in range(5))
    held, sems = refs[5 * GROUPS : 5 * GROUPS + 12], refs[5 * GROUPS + 12 :]
    (
        halo_send, halo_recv, core_send, core_recv, xy_send, xy_recv, z_send, z_recv,
        ag_send, ag_recv, fw_send, fw_recv, out_sem, in_sem,
    ) = sems
    loads = [
        pltpu.make_async_copy(there, here, in_sem.at[i])
        for i, (there, here) in enumerate(
            zip((tok, ct, qkv1, proj1, up1, dn1, bias1, qkv2, proj2, up2, dn2, bias2), held)
        )
    ]
    for i in (0, 2, 6, 1, 3, 4, 5, 7, 11, 8, 9, 10):
        loads[i].start()
    tok, ct, qkv1, proj1, up1, dn1, bias1, qkv2, proj2, up2, dn2, bias2 = held
    lon = lax.axis_index("lon")
    lat = lax.axis_index("lat")
    core = lax.rem(lon, 2)
    chip = lon // 2
    y_hi = lat // 8
    zi = lax.rem(lat, 8)
    me_xy = y_hi * 8 + chip

    def sibling():
        return {"lon": chip * 2 + 1 - core, "lat": lat}

    def xy_dev(j):
        return {"lon": lax.rem(j, 8) * 2 + core, "lat": (j // 8) * 8 + zi}

    def z_dev(j):
        return {"lon": lon, "lat": y_hi * 8 + j}

    def near(step_lon, step_lat):
        return {
            "lon": lax.rem(lon + step_lon + 16, 16),
            "lat": lax.rem(lat + step_lat + 16, 16),
        }

    barrier = pltpu.get_barrier_semaphore()

    def greet(device):
        pl.semaphore_signal(barrier, inc=1, device_id=device, device_id_type=MESH)

    greet(sibling())
    for k in range(1, 16):
        greet(xy_dev(lax.rem(me_xy + k, 16)))
    for k in range(1, 8):
        greet(z_dev(lax.rem(zi + k, 8)))
    for s in (1, -1):
        greet(near(s, 0))
        greet(near(0, s))
        greet(near(s, s))

    def halo_copy(x, part, step):
        first, count = HALO_PARTS[part]
        device = near(step if part != 1 else 0, step if part != 0 else 0)
        return pltpu.make_async_remote_copy(
            src_ref=halo_out.at[x, pl.ds(first, count)],
            dst_ref=halo_in.at[x, pl.ds(first, count)],
            send_sem=halo_send.at[x, part],
            recv_sem=halo_recv.at[x, part],
            device_id=device,
            device_id_type=MESH,
        )

    def halo_start(x, src, step, parts=(0, 1, 2)):
        if step > 0:
            where = (range(0, 9), range(9, 12), (0, 6, 12), (18,))
        else:
            where = (range(3, 12), range(0, 3), (6, 12, 18), (0,))
        pack_halo(src, pack, halo_out.at[x], *where, parts)
        for part in parts:
            halo_copy(x, part, step).start()

    def halo_finish(x, src, dst, step, windows=(0, 1, 2, 3)):
        for part in range(3):
            halo_copy(x, part, step).wait()
        outside = jnp.where(lat == (0 if step > 0 else 15), 0.0, 1.0).astype(F32)
        halo_f[0:112, :] = halo_in[x, 0:112].astype(F32)
        halo_f[112:, :] = halo_in[x, 112:].astype(F32) * outside
        unpack_shift(src, halo_f, dst, step, windows)

    limit = 16 * 12 - PAD
    starts = (lat * 12, lat * 12 - 3)
    weights = (
        (ga1, qkv1, proj1, gm1, up1, dn1, bias1),
        (ga2, qkv2, proj2, gm2, up2, dn2, bias2),
    )

    def prepare(b):
        ga, wqkv, wproj, gm, wup, wdn, bias = weights[b]
        wp[b] = jnp.zeros((D, 768), BF16)
        for i in range(3):
            part = wqkv[...].astype(F32)[:, D * i : D * i + D]
            wp[b, :, 256 * i : 256 * i + D] = part.astype(BF16)
        rows_i = lax.broadcasted_iota(jnp.int32, (WIN, WIN), 0)
        cols_i = lax.broadcasted_iota(jnp.int32, (WIN, WIN), 1)
        eye = jnp.where(rows_i == cols_i, 1.0, 0.0).astype(F32).astype(BF16)
        for wr in range(2):
            here = live_column(starts[b] + 6 * wr, limit)
            penalty = (here - 1.0) * 30000.0
            for wc in range(2):
                alive[b, (2 * wr + wc) * WIN : (2 * wr + wc + 1) * WIN, :] = here
            bt[wr, :, 0:864] = dot_nt(eye, bias[wr]) + penalty
            bt[wr, :, 864:] = jnp.zeros((WIN, STACK - 864), F32)

    def block_forward(b, x_in, x_out, lo, hi):
        ga, wqkv, wproj, gm, wup, wdn, bias = weights[b]
        gain_a = ga[...].reshape(1, D)
        gain_m = gm[...].reshape(1, D)

        span = slice(lo * WIN, hi * WIN)

        def f_qkv():
            xh, r = normalise(x_in[span, :], True)
            xhat1[b, span, :] = xh
            r1[b, span, :] = r
            normed[b, span, :] = (xh * gain_a).astype(BF16)
            proj_all[b, span, :] = dot_nn(normed[b, span, :], wp[b]).astype(BF16)

        stage("f_qkv", f_qkv)

        def f_att(w):
            rows = win_rows(w)
            wr = w // 2
            q = proj_all[b, rows, 0:D]
            k = proj_all[b, rows, 256 : 256 + D]
            v = proj_all[b, rows, 512 : 512 + D]
            for h in range(HEADS):
                qm[b, w, WIN * h : WIN * h + WIN, :] = q * head_mask(h, BF16)
            qm[b, w, 864:, :] = jnp.zeros((STACK - 864, D), BF16)
            for c0, c1 in CHUNKS:
                s = dot_nt(k, qm[b, w, c0:c1, :]) * SCALE + bt[wr, :, c0:c1]
                e = jnp.exp(s - jnp.max(s, axis=0, keepdims=True))
                total = jnp.sum(e, axis=0, keepdims=True)
                pt[b, w, :, c0:c1] = (e * (1.0 / total)).astype(BF16)
            o = dot_tn(pt[b, w], v)
            a = own_lanes(o)
            att[b, rows, :] = a.astype(BF16)

        stage("f_att", lambda: [f_att(w) for w in range(lo, hi)])

        def f_mlp():
            resid = x_in[span, :] + dot_nn(att[b, span, :], wproj[...])
            x_out[span, :] = resid
            xh, r = normalise(resid, False)
            xhat2[b, span, :] = xh
            r2[b, span, :] = r
            second[b, span, :] = (xh * gain_m).astype(BF16)
            c = math.sqrt(2.0 / math.pi)
            for n in range(3):
                at = slice(256 * n, 256 * n + 256)
                u = dot_nn(second[b, span, :], wup[:, at])
                u2 = u * u
                t = jnp.tanh(u * (c + (c * 0.044715) * u2))
                half = 0.5 + 0.5 * t
                hidden[b, span, at] = (u * half).astype(BF16)
                slope = half + u * (half * (1.0 - half)) * (2 * c + (6 * c * 0.044715) * u2)
                gp[b, span, at] = slope.astype(BF16)
            out = (x_out[span, :] + dot_nt(hidden[b, span, :], wdn[...])) * alive[b, span, :]
            x_out[span, :] = out.astype(BF16).astype(F32)

        stage("f_mlp", f_mlp)

    def mlp_backward(b, d_out, lo, hi):
        ga, wqkv, wproj, gm, wup, wdn, bias = weights[b]
        gain_m = gm[...].reshape(1, D)

        span = slice(lo * WIN, hi * WIN)

        def b_mlp():
            dtb = (d_out[span, :] * alive[b, span, :]).astype(BF16)
            dtot[span, :] = dtb
            for n in range(3):
                at = slice(256 * n, 256 * n + 256)
                dh = dot_nn(dtot[span, :], wdn[:, at]).astype(BF16).astype(F32)
                du[span, at] = (dh * gp[b, span, at].astype(F32)).astype(BF16)
            dy = dot_nt(du[span, :], wup[...]).astype(BF16).astype(F32) * gain_m
            dr = dtot[span, :].astype(F32) + normalise_back(dy, xhat2[b, span, :], r2[b, span, :])
            dres[span, :] = dr
            dres_b[span, :] = dr.astype(BF16)
            datt[span, :] = dot_nt(dres_b[span, :], wproj[...]).astype(BF16)

        stage("b_mlp", b_mlp)

    def attention_backward(b, lo, hi, between=None):
        def b_att(w):
            rows = win_rows(w)
            k = proj_all[b, rows, 256 : 256 + D]
            v = proj_all[b, rows, 512 : 512 + D]
            do = datt[rows, :]
            for h in range(HEADS):
                dom[w, WIN * h : WIN * h + WIN, :] = do * head_mask(h, BF16)
            dom[w, 864:, :] = jnp.zeros((STACK - 864, D), BF16)
            for c0, c1 in CHUNKS:
                dp = dot_nt(v, dom[w, c0:c1, :]).astype(BF16).astype(F32)
                p = pt[b, w, :, c0:c1].astype(F32)
                delta = jnp.sum(p * dp, axis=0, keepdims=True)
                dst_[w, :, c0:c1] = (p * (dp - delta)).astype(BF16)
            zeros = jnp.zeros((WIN, 64), BF16)
            dqkv[rows, 512 : 512 + D] = dot_nn(pt[b, w], dom[w]).astype(BF16)
            dqkv[rows, 256 : 256 + D] = (dot_nn(dst_[w], qm[b, w]) * SCALE).astype(BF16)
            o = dot_tn(dst_[w], k)
            a = own_lanes(o)
            dqkv[rows, 0:D] = (a * SCALE).astype(BF16)
            for i in range(3):
                dqkv[rows, 256 * i + D : 256 * i + 256] = zeros

            if between is not None:
                between(w)

        stage("b_att", lambda: [b_att(w) for w in range(lo, hi)])

    def input_backward(b, d_in, lo, hi):
        gain_a = weights[b][0][...].reshape(1, D)

        span = slice(lo * WIN, hi * WIN)

        def b_qkv():
            dy = dot_nt(dqkv[span, :], wp[b]).astype(BF16).astype(F32) * gain_a
            dx = dres[span, :] + normalise_back(dy, xhat1[b, span, :], r1[b, span, :])
            d_in[span, :] = dx.astype(BF16).astype(F32)

        stage("b_qkv", b_qkv)

    def put(gr, at, matrix):
        for i in range(matrix.shape[1] // 128):
            rows = slice((at + i) * D, (at + i + 1) * D)
            gs[gr][rows, :] = matrix[:, 128 * i : 128 * i + 128].astype(BF16)

    def mlp_terms(b, gr):
        put(gr, 0, dot_tn(second[b], du[...]))
        put(gr, 6, dot_tn(dtot[...], hidden[b]))
        pr = dot_tn(att[b], dres_b[...])
        put(gr, 12, pr[:, 0:128])
        w5[b, :, 576:640] = pr[:, 128:D]

    def attention_terms(b, gr):
        terms = dot_tn(normed[b], dqkv[...])
        for i in range(3):
            w5[b, :, D * i : D * i + D] = terms[:, 256 * i : 256 * i + D]
        put(gr, 0, w5[b])

    def remote(src, dst, send, recv, device):
        return pltpu.make_async_remote_copy(
            src_ref=src, dst_ref=dst, send_sem=send, recv_sem=recv,
            device_id=device, device_id_type=MESH,
        )

    def piece_at(gr, j):
        return pl.ds(pl.multiple_of(j * PIECES[gr], 16), PIECES[gr])

    def f_at(gr, c, j):
        return pl.ds(pl.multiple_of(BASES[gr] + (c * 16 + j) * PIECES[gr], 16), PIECES[gr])

    def core_copy(gr):
        rows = 16 * PIECES[gr]
        there = pl.ds(pl.multiple_of((1 - core) * rows, 16), rows)
        return remote(gs[gr].at[there], r0s[gr], core_send.at[gr], core_recv.at[gr], sibling())

    def half_at(gr, c):
        rows = 16 * PIECES[gr]
        return pl.ds(pl.multiple_of(BASES[gr] + c * rows, 16), rows)

    def xy_copy(gr, k):
        j = lax.rem(me_xy + k, 16)
        return remote(
            hhs[gr].at[piece_at(gr, j)], rrs[gr].at[k - 1],
            xy_send.at[gr], xy_recv.at[gr], xy_dev(j),
        )

    def xy_all(gr):
        every = rrs[gr].at[pl.ds(0, 15)]
        return remote(every, every, xy_send.at[gr], xy_recv.at[gr], xy_dev(lax.rem(me_xy + 1, 16)))

    def z_copy(gr, k):
        here = zs[gr].at[zi]
        return remote(here, here, z_send.at[gr], z_recv.at[gr], z_dev(lax.rem(zi + k, 8)))

    def z_all(gr):
        every = zs[gr].at[pl.ds(0, 7)]
        return remote(every, every, z_send.at[gr], z_recv.at[gr], z_dev(lax.rem(zi + 1, 8)))

    def ag_copy(gr, k):
        here = f.at[f_at(gr, core, me_xy)]
        return remote(here, here, ag_send.at[gr], ag_recv.at[gr], xy_dev(lax.rem(me_xy + k, 16)))

    def ag_all(gr):
        every = f.at[pl.ds(BASES[gr], 15 * PIECES[gr])]
        return remote(every, every, ag_send.at[gr], ag_recv.at[gr], xy_dev(lax.rem(me_xy + 1, 16)))

    def fw_copy(gr, c):
        half = f.at[half_at(gr, c)]
        return remote(half, half, fw_send.at[gr], fw_recv.at[gr], sibling())

    def each(count, body):
        def step(k, carry):
            body(k)
            return carry
        lax.fori_loop(1, count, step, 0)

    def sum_0(gr):
        core_copy(gr).start()

    def sum_1(gr):
        core_copy(gr).wait()

        def add(j):
            own = gs[gr][pl.ds(pl.multiple_of((core * 16 + j) * PIECES[gr], 16), PIECES[gr]), :]
            there = r0s[gr][piece_at(gr, j), :]
            hhs[gr][piece_at(gr, j), :] = (own.astype(F32) + there.astype(F32)).astype(BF16)

        def add_and_send(k):
            add(lax.rem(me_xy + k, 16))
            xy_copy(gr, k).start()

        each(16, add_and_send)
        add(me_xy)

    def sum_2(gr):
        total = hhs[gr][piece_at(gr, me_xy), :].astype(F32)
        xy_all(gr).wait_recv()
        for k in range(15):
            total = total + rrs[gr][k].astype(F32)
        zs[gr][zi] = total.astype(BF16)
        each(8, lambda k: z_copy(gr, k).start())

    def sum_3(gr):
        z_all(gr).wait_recv()
        total = zs[gr][0].astype(F32)
        for j in range(1, 8):
            total = total + zs[gr][j].astype(F32)
        f[f_at(gr, core, me_xy), :] = total.astype(BF16)
        each(16, lambda k: ag_copy(gr, k).start())

    def sum_4(gr):
        ag_all(gr).wait_recv()
        fw_copy(gr, core).start()

    def sum_5(gr):
        fw_copy(gr, 1 - core).wait_recv()

    def sum_sent(gr):
        xy_all(gr).wait_send()
        z_all(gr).wait_send()
        ag_all(gr).wait_send()
        fw_copy(gr, core).wait_send()

    def out_copy(gr):
        at = pl.ds(BASES[gr], 32 * PIECES[gr])
        return pltpu.make_async_copy(f.at[at], f_o.at[at], out_sem.at[gr])

    def aside(w):
        if w == 1:
            sum_1(2)

    def field_copy(i):
        return pltpu.make_async_copy((res_v, gt_v)[i], (res_o, gt_o)[i], out_sem.at[GROUPS + i])

    for gr in range(GROUPS):
        used = (13, 5)[gr % 2] * D
        gs[gr][used:, :] = jnp.zeros((32 * PIECES[gr] - used, 128), BF16)
    loads[0].wait()
    tile_to_windows(tok, cur)
    loads[2].wait()
    loads[6].wait()
    stage("prepare", lambda: prepare(0))
    for i in (3, 4, 5):
        loads[i].wait()
    block_forward(0, cur, nxt, 2, 4)
    pl.semaphore_wait(barrier, 29)
    halo_start(1, nxt, 1, (1, 2))
    block_forward(0, cur, nxt, 0, 2)
    halo_start(1, nxt, 1, (0,))
    loads[1].wait()
    tile_to_windows(ct, cw)
    halo_start(0, cw, 1)
    for i in (7, 8, 9, 10, 11):
        loads[i].wait()
    stage("prepare", lambda: prepare(1))
    unpack_shift(nxt, halo_f, cur, 1, (3,))
    block_forward(1, cur, out2, 3, 4)
    halo_finish(1, nxt, cur, 1, (0, 1, 2))
    block_forward(1, cur, out2, 0, 3)
    halo_start(2, out2, -1)
    halo_finish(0, cw, cur, 1)
    mlp_backward(1, cur, 0, 4)
    stage("mlp_terms", lambda: mlp_terms(1, 0))
    sum_0(0)
    attention_backward(1, 0, 2)
    input_backward(1, cw, 0, 2)
    halo_start(3, cw, -1, (1, 2))
    attention_backward(1, 2, 3)
    input_backward(1, cw, 2, 3)
    halo_start(3, cw, -1, (0,))
    sum_1(0)
    attention_backward(1, 3, 4)
    input_backward(1, cw, 3, 4)
    stage("attention_terms", lambda: attention_terms(1, 1))
    sum_0(1)
    unpack_shift(cw, halo_f, nxt, -1, (0,))
    mlp_backward(0, nxt, 0, 1)
    sum_1(1)
    halo_finish(3, cw, nxt, -1, (1, 2, 3))
    mlp_backward(0, nxt, 1, 4)
    stage("mlp_terms", lambda: mlp_terms(0, 2))
    sum_0(2)
    sum_2(0)
    attention_backward(0, 0, 4, aside)
    stage("attention_terms", lambda: attention_terms(0, 3))
    sum_0(3)
    input_backward(0, cur, 0, 4)
    sum_1(3)
    windows_to_tile(cur, gt_v)
    field_copy(1).start()
    sum_2(1)
    halo_finish(2, out2, nxt, -1)
    windows_to_tile(nxt, res_v)
    field_copy(0).start()
    sum_3(0)
    sum_2(2)
    sum_3(1)
    sum_2(3)
    sum_4(0)
    sum_3(2)
    sum_4(1)
    sum_3(3)
    sum_5(0)
    out_copy(0).start()
    sum_4(2)
    sum_5(1)
    out_copy(1).start()
    sum_4(3)
    sum_5(2)
    out_copy(2).start()
    sum_5(3)
    out_copy(3).start()
    for gr in range(GROUPS):
        sum_sent(gr)
        out_copy(gr).wait()
    field_copy(0).wait()
    field_copy(1).wait()


def unpack_kernel(factor, f_in, res, gt, res_o, gt_o, *refs):
    outs, f, held, sems = refs[:8], refs[8], refs[9:17], refs[17]
    res_v, gt_v = refs[18], refs[19]
    copies = []
    fields = [
        pltpu.make_async_copy(res, res_v, sems.at[0]),
        pltpu.make_async_copy(gt, gt_v, sems.at[1]),
    ]
    parts = []
    for gr in range(GROUPS):
        at = pl.ds(BASES[gr], 32 * PIECES[gr])
        parts.append(pltpu.make_async_copy(f_in.at[at], f.at[at], sems.at[2 + gr]))
    for copy in parts + fields:
        copy.start()

    def tile(gr, i):
        at = BASES[gr] + i * D
        return f[at : at + D, :].astype(F32) * factor

    def mlp_out(gr, up, down, proj):
        for n in range(6):
            up[:, 128 * n : 128 * n + 128] = tile(gr, n)
            down[:, 128 * n : 128 * n + 128] = tile(gr, n + 6)
        proj[:, 0:128] = tile(gr, 12)

    def attention_out(gr, qkv, proj):
        for n in range(4):
            qkv[:, 128 * n : 128 * n + 128] = tile(gr, n)
        last = tile(gr, 4)
        qkv[:, 512:576] = last[:, 0:64]
        proj[:, 128:D] = last[:, 64:128]

    def send(first, count):
        for i in range(first, first + count):
            copy = pltpu.make_async_copy(held[i], outs[i], sems.at[2 + GROUPS + i])
            copy.start()
            copies.append(copy)

    parts[0].wait()
    mlp_out(0, held[6], held[7], held[5])
    send(6, 2)
    for i, (held_f, out_f) in enumerate(((res_v, res_o), (gt_v, gt_o))):
        fields[i].wait()
        copy = pltpu.make_async_copy(held_f, out_f, sems.at[i])
        copy.start()
        copies.append(copy)
    parts[1].wait()
    attention_out(1, held[4], held[5])
    send(4, 2)
    parts[2].wait()
    mlp_out(2, held[2], held[3], held[1])
    send(2, 2)
    parts[3].wait()
    attention_out(3, held[0], held[1])
    send(0, 2)
    for copy in copies:
        copy.wait()


def body(
    tokens, ga1, qkv1, proj1, gm1, up1, dn1, bias1,
    ga2, qkv2, proj2, gm2, up2, dn2, bias2, cotangent,
):
    vmem = pl.BlockSpec(memory_space=pltpu.VMEM)
    tile = jax.ShapeDtypeStruct((24, 24, D), BF16)

    def dma(*shape):
        return pltpu.SemaphoreType.DMA(shape)

    big = (
        tokens.reshape(24, 24, D), cotangent.reshape(24, 24, D),
        qkv1, proj1, up1, dn1.T, bias1.reshape(2, HEADS * WIN, WIN),
        qkv2, proj2, up2, dn2.T, bias2.reshape(2, HEADS * WIN, WIN),
    )
    anywhere = pl.BlockSpec(memory_space=pl.ANY)
    scratch = [
        pltpu.VMEM((2, D, 768), BF16),
        pltpu.VMEM((2, WIN, STACK), F32),
        pltpu.VMEM((2, 576, 1), F32),
        pltpu.VMEM((2, 576, D), F32),
        pltpu.VMEM((2, 576, D), F32),
        pltpu.VMEM((2, 576, D), BF16),
        pltpu.VMEM((2, 576, 768), BF16),
        pltpu.VMEM((2, 4, STACK, D), BF16),
        pltpu.VMEM((2, 4, WIN, STACK), BF16),
        pltpu.VMEM((2, 576, D), BF16),
        pltpu.VMEM((2, 576, D), F32),
        pltpu.VMEM((2, 576, D), F32),
        pltpu.VMEM((2, 576, D), BF16),
        pltpu.VMEM((2, 576, 768), BF16),
        pltpu.VMEM((2, 576, 768), BF16),
        pltpu.VMEM((24, 24, D), BF16),
        pltpu.VMEM((24, 24, D), BF16),
        pltpu.VMEM((ROWS, 128), BF16),
        pltpu.VMEM((576, D), F32),
        pltpu.VMEM((576, D), F32),
        pltpu.VMEM((576, D), F32),
        pltpu.VMEM((576, D), F32),
        pltpu.VMEM((HALO_ROWS, D), F32),
        pltpu.VMEM((HALO_ROWS, D), F32),
        pltpu.VMEM((4, HALO_ROWS, D), BF16),
        pltpu.VMEM((4, HALO_ROWS, D), BF16),
        pltpu.VMEM((576, D), BF16),
        pltpu.VMEM((576, 768), BF16),
        pltpu.VMEM((576, D), F32),
        pltpu.VMEM((576, D), BF16),
        pltpu.VMEM((576, D), BF16),
        pltpu.VMEM((4, STACK, D), BF16),
        pltpu.VMEM((4, WIN, STACK), BF16),
        pltpu.VMEM((576, 768), BF16),
        pltpu.VMEM((2, D, 640), F32),
        *[pltpu.VMEM((32 * r, 128), BF16) for r in PIECES],
        *[pltpu.VMEM((16 * r, 128), BF16) for r in PIECES],
        *[pltpu.VMEM((16 * r, 128), BF16) for r in PIECES],
        *[pltpu.VMEM((16, r, 128), BF16) for r in PIECES],
        *[pltpu.VMEM((8, r, 128), BF16) for r in PIECES],
        *[pltpu.VMEM(a.shape, BF16) for a in big],
        dma(4, 3), dma(4, 3),
        dma(GROUPS), dma(GROUPS),
        dma(GROUPS), dma(GROUPS),
        dma(GROUPS), dma(GROUPS),
        dma(GROUPS), dma(GROUPS),
        dma(GROUPS), dma(GROUPS),
        dma(GROUPS + 2), dma(12),
    ]
    res, gt, f = pl.pallas_call(
        megakernel,
        out_shape=(tile, tile, jax.ShapeDtypeStruct((ROWS, 128), BF16)),
        in_specs=[vmem] * 4 + [anywhere] * 12,
        out_specs=(anywhere,) * 3,
        scratch_shapes=scratch,
        compiler_params=pltpu.CompilerParams(
            collective_id=0, has_side_effects=True, vmem_limit_bytes=60 * 1024 * 1024
        ),
    )(
        ga1, gm1, ga2, gm2, *big
    )
    one = [
        jax.ShapeDtypeStruct((D, 3 * D), F32),
        jax.ShapeDtypeStruct((D, D), F32),
        jax.ShapeDtypeStruct((D, 4 * D), F32),
        jax.ShapeDtypeStruct((D, 4 * D), F32),
    ]
    outs = list(pl.pallas_call(
        functools.partial(unpack_kernel, 1.0 / math.sqrt(256.0 * 576.0)),
        out_shape=[tile, tile] + one + one,
        in_specs=[anywhere] * 3,
        out_specs=[anywhere] * 10,
        scratch_shapes=[pltpu.VMEM((ROWS, 128), BF16)]
        + [pltpu.VMEM(s.shape, F32) for s in one + one]
        + [dma(10 + GROUPS), pltpu.VMEM(tile.shape, BF16), pltpu.VMEM(tile.shape, BF16)],
        compiler_params=pltpu.CompilerParams(vmem_limit_bytes=60 * 1024 * 1024),
    )(f, res, gt))
    shape = (2, 12, 24, D)
    terms = outs[2:5] + [outs[5].T] + outs[6:9] + [outs[9].T]
    return (outs[0].reshape(shape), outs[1].reshape(shape)) + tuple(terms)


def solution(mesh):
    grid = P(None, "lat", "lon", None)
    bias = P("lat", None, None, None, None)
    block = (P(), P(), P(), P(), P(), P(), bias)
    return jax.shard_map(
        body,
        mesh=mesh,
        in_specs=(grid,) + block + block + (grid,),
        out_specs=(grid, grid) + (P(),) * 8,
        check_vma=False,
    )
```
